32 devices in a mesh: ctx: 8 (over z, y), head: 4 (over x, core).
Axes of the slice: x: 2, y: 2, z: 4, core: 2. Of those that a mesh axis runs over, the one named last changes fastest.
Arguments:
- queries: bfloat16 [4096, 2048], P('ctx', 'head'), may hold values from -6 to 6
- keys: bfloat16 [4096, 2048], P('ctx', 'head'), may hold values from -6 to 6
- values: bfloat16 [4096, 2048], P('ctx', 'head'), may hold values from -16 to 16
- out_grad: bfloat16 [4096, 2048], P('ctx', 'head'), may hold values from -6 to 6
- norm_gain: float32 [2048], P('head'), may hold values from 0.1 to 1.9
- doc_lengths: int32 [16], replicated, may hold values from 1 to 2048, 4096 in all
- group_level: int32 [4], replicated, may hold values from 0 to 2
Outputs:
- output: bfloat16 [4096, 2048], P('ctx', 'head')
- query_grad: bfloat16 [4096, 2048], P('ctx', 'head')
- key_grad: bfloat16 [4096, 2048], P('ctx', 'head')
- value_grad: bfloat16 [4096, 2048], P('ctx', 'head')
The draws below stay inside these ranges and needn't reach their ends.
All inputs are finite; a program needn't handle non-finite values.
Results may differ from the reference program's by a relative error of at most 0.013.
Values may be sent and summed in bfloat16 or wider, within the bound.
A program may use at most 64 MiB of HBM per device.

```python
import math
import jax
import jax.numpy as jnp
import numpy as np
from jax import lax

HEAD_FEATURES = 128
HEAD_DEV = 4
SEGMENT = 512
DILATION = 32
DOCS = 16
SEQUENCE_TOKENS = 4096
HEADS = 16
WIDTH = 2048
GROUPS = 4
SELECTED = 128
DOC_MOST = 2048


def draw_queries(key, part):
    drawn = jnp.clip(jax.random.normal(jax.random.fold_in(key, 1), (SEQUENCE_TOKENS, WIDTH), jnp.float32), -6.0, 6.0)
    return drawn.astype(jnp.bfloat16)


def draw_keys(key, part):
    drawn = jnp.clip(jax.random.normal(jax.random.fold_in(key, 2), (SEQUENCE_TOKENS, WIDTH), jnp.float32), -6.0, 6.0)
    return drawn.astype(jnp.bfloat16)


def draw_values(key, part):
    head_of = jnp.arange(WIDTH) // HEAD_FEATURES
    ramp = head_of.astype(jnp.float32) / max(HEADS - 1, 1)
    drawn = jnp.clip(jax.random.normal(jax.random.fold_in(key, 5), (SEQUENCE_TOKENS, WIDTH), jnp.float32), -4.0, 4.0)
    return (drawn * (0.6 + 1.2 * ramp)).astype(jnp.bfloat16)


def with_ends(values, own_key, least, top_value):
    spot = [jax.random.randint(jax.random.fold_in(own_key, axis), (), 0, length) for axis, length in enumerate(values.shape)]
    main_axis = values.shape.index(max(values.shape))
    neighbour = spot[:main_axis] + [(spot[main_axis] + 1) % values.shape[main_axis]] + spot[main_axis + 1:]
    return values.at[tuple(spot)].set(least).at[tuple(neighbour)].set(top_value)


def shard_levels(rng, shape, pieces, low, high):
    loudness = 1.0
    for position, blocks in pieces:
        heights = jax.random.uniform(jax.random.fold_in(jax.random.fold_in(rng, 6), position), (blocks,), jnp.float32, low / len(pieces), high / len(pieces))
        loudness = loudness * jnp.repeat(jnp.exp(heights), shape[position] // blocks).reshape((-1,) + (1,) * (len(shape) - 1 - position))
    return loudness


def split_up(number_of, total, reach, slope):
    portions = [(1 << 20) // math.isqrt(rank ** slope) + 1 for rank in range(2, number_of + 1)]
    spare, counts = total - reach - (number_of - 1), [1] * (number_of - 1)
    while spare > 0:
        movable = [i for i in range(number_of - 1) if counts[i] < reach]
        mass, budget = sum([portions[i] for i in movable]), spare
        for i in movable:
            more = min(reach - counts[i], max(1, budget * portions[i] // mass), spare)
            counts[i] = counts[i] + more
            spare = spare - more
    return np.array([reach] + counts)


def uneven(own_key, number_of, total, reach, slope):
    if number_of == 2:
        one = jax.random.randint(own_key, (), max(1, total - reach), min(reach, total - 1) + 1)
        return jnp.stack([one, total - one])
    sizes = jnp.asarray(split_up(number_of, total, reach, slope), jnp.int32)
    couples = (number_of - 1) // 2
    giver, taker = sizes[1:1 + 2 * couples:2], sizes[2:2 + 2 * couples:2]
    slack = jnp.minimum(giver - 1, reach - taker)
    shifted = jax.random.randint(jax.random.fold_in(own_key, 1), (couples,), 0, 1 << 20) % (slack + 1)
    sizes = sizes.at[1:1 + 2 * couples:2].set(giver - shifted).at[2:2 + 2 * couples:2].set(taker + shifted)
    return sizes[jax.random.permutation(jax.random.fold_in(own_key, 2), number_of)]


def normal_values(key, dims, deviation, limit, cuts=(), kind=jnp.bfloat16):
    array = deviation * jax.random.normal(key, dims, jnp.float32)
    if cuts:
        array = array * shard_levels(key, dims, cuts, -0.22, 0.18)
    return jnp.clip(array, -limit, limit).astype(kind)


def setup_inputs(seed: int = 0) -> dict:
    arg_keys = jax.random.split(jax.random.key(seed), 8)
    return {
        "queries": draw_queries(jax.random.fold_in(arg_keys[7], 71), 0),
        "keys": draw_keys(jax.random.fold_in(arg_keys[7], 71), 0),
        "values": draw_values(jax.random.fold_in(arg_keys[7], 71), 0),
        "out_grad": normal_values(arg_keys[3], (SEQUENCE_TOKENS, WIDTH), 1.0, 6.0, ((0, 8), (1, 4))),
        "norm_gain": jnp.clip(1.0 + 0.18 * jax.random.normal(arg_keys[4], (WIDTH,), jnp.float32), 0.1, 1.9),
        "doc_lengths": uneven(arg_keys[5], DOCS, SEQUENCE_TOKENS, DOC_MOST, 2).astype(jnp.int32),
        "group_level": with_ends(jax.random.randint(arg_keys[6], (GROUPS,), 0, 3), jax.random.fold_in(arg_keys[6], 1), 0, 2).astype(jnp.int32),
    }


EPS = 1e-05

def document_of(places, doc_lengths):
    ends = jnp.cumsum(doc_lengths, dtype=jnp.int32)
    return lax.optimization_barrier(jnp.sum((places[..., None] >= ends).astype(jnp.int32), axis=-1, dtype=jnp.int32))

def head_masks(head, doc_lengths, group_level):
    offset = (head % DILATION).astype(jnp.int32)
    rate = jnp.left_shift(jnp.int32(1), group_level[head // HEAD_DEV].astype(jnp.int32))
    places = jnp.arange(SEQUENCE_TOKENS, dtype=jnp.int32)
    docs = document_of(places, doc_lengths)
    counter = jnp.arange(SELECTED, dtype=jnp.int32)
    far_places = counter * DILATION + offset
    far_docs = document_of(far_places, doc_lengths)
    local_places = places.reshape(SEQUENCE_TOKENS // SEGMENT, SEGMENT)
    local_docs = docs.reshape(SEQUENCE_TOKENS // SEGMENT, SEGMENT)
    near_mask = (local_places[:, :, None] >= local_places[:, None, :]) & (local_docs[:, :, None] == local_docs[:, None, :])
    far_mask = (far_places[None, :] <= places[:, None]) & (far_docs[None, :] == docs[:, None]) & (counter % rate == 0)[None, :]
    return (offset, near_mask, far_mask.reshape(SEQUENCE_TOKENS // SEGMENT, SEGMENT, SELECTED))

def pick_rows(rows, offset):
    return lax.dynamic_index_in_dim(rows.reshape(SELECTED, DILATION, HEAD_FEATURES), offset, axis=1, keepdims=False)

def weights_of(query_head, key_head, head, doc_lengths, group_level):
    offset, near_mask, far_mask = head_masks(head, doc_lengths, group_level)
    logit_scale = HEAD_FEATURES ** (-0.5)
    query_tiles = query_head.reshape(SEQUENCE_TOKENS // SEGMENT, SEGMENT, HEAD_FEATURES)
    key_tiles = key_head.reshape(SEQUENCE_TOKENS // SEGMENT, SEGMENT, HEAD_FEATURES)
    far_keys = pick_rows(key_head, offset)
    nearby_logit = jnp.einsum('vlr,vwr->vlw', query_tiles.astype(jnp.float32), key_tiles.astype(jnp.float32)) * logit_scale
    far_score = jnp.dot(query_head, far_keys.T, preferred_element_type=jnp.float32).reshape(SEQUENCE_TOKENS // SEGMENT, SEGMENT, SELECTED) * logit_scale
    top = jnp.maximum(lax.optimization_barrier(jnp.max(jnp.where(near_mask, nearby_logit, -jnp.inf), -1)), lax.optimization_barrier(jnp.max(jnp.where(far_mask, far_score, -jnp.inf), -1)))
    summed = lax.optimization_barrier(jnp.sum(jnp.where(near_mask, jnp.exp(nearby_logit - top[..., None]), 0.0), -1)) + lax.optimization_barrier(jnp.sum(jnp.where(far_mask, jnp.exp(far_score - top[..., None]), 0.0), -1))
    log_total = top + jnp.log(summed)
    nearby_weight = jnp.where(near_mask, jnp.exp(nearby_logit - log_total[..., None]), 0.0)
    far_weight = jnp.where(far_mask, jnp.exp(far_score - log_total[..., None]), 0.0)
    return (nearby_weight, far_weight, offset)

def reference(queries, keys, values, out_grad, norm_gain, doc_lengths, group_level):
    logit_scale = HEAD_FEATURES ** (-0.5)

    def split(rows):
        return rows.reshape(SEQUENCE_TOKENS, HEADS, HEAD_FEATURES).transpose(1, 0, 2)

    def merge(rows):
        return rows.transpose(1, 0, 2).reshape(SEQUENCE_TOKENS, WIDTH)

    def forward_head(inputs):
        query_head, key_head, value_head, head = inputs
        nearby_weight, far_weight, offset = weights_of(query_head, key_head, head, doc_lengths, group_level)
        value_tiles = value_head.reshape(SEQUENCE_TOKENS // SEGMENT, SEGMENT, HEAD_FEATURES)
        far_values = pick_rows(value_head, offset)
        nearby_portion = jnp.einsum('xen,xna->xea', nearby_weight.astype(jnp.bfloat16).astype(jnp.float32), value_tiles.astype(jnp.float32)).reshape(SEQUENCE_TOKENS, HEAD_FEATURES)
        far_part = jnp.dot(far_weight.reshape(SEQUENCE_TOKENS, SELECTED).astype(jnp.bfloat16), far_values, preferred_element_type=jnp.float32)
        return (nearby_portion + far_part).astype(jnp.bfloat16)
    head_ids = jnp.arange(HEADS, dtype=jnp.int32)
    attended = merge(lax.map(forward_head, (split(queries), split(keys), split(values), head_ids)))
    flat = attended.astype(jnp.float32)
    mean = lax.optimization_barrier(jnp.sum(flat, 1)) / WIDTH
    rstd = lax.rsqrt(lax.optimization_barrier(jnp.sum(flat * flat, 1)) / WIDTH - mean * mean + EPS)
    normed = (flat - mean[:, None]) * rstd[:, None]
    output = (normed * norm_gain).astype(jnp.bfloat16)
    scaled = out_grad.astype(jnp.float32) * norm_gain
    grad_mean = lax.optimization_barrier(jnp.sum(scaled, 1)) / WIDTH
    grad_proj = lax.optimization_barrier(jnp.sum(scaled * normed, 1)) / WIDTH
    att_grad = (rstd[:, None] * (scaled - grad_mean[:, None] - normed * grad_proj[:, None])).astype(jnp.bfloat16)

    def backward_head(inputs):
        query_head, key_head, value_head, attended_head, grad_head, head = inputs
        nearby_weight, far_weight, offset = weights_of(query_head, key_head, head, doc_lengths, group_level)
        blocks = SEQUENCE_TOKENS // SEGMENT
        query_tiles = query_head.reshape(blocks, SEGMENT, HEAD_FEATURES).astype(jnp.float32)
        key_tiles = key_head.reshape(blocks, SEGMENT, HEAD_FEATURES).astype(jnp.float32)
        value_tiles = value_head.reshape(blocks, SEGMENT, HEAD_FEATURES).astype(jnp.float32)
        gradient_tiles = grad_head.reshape(blocks, SEGMENT, HEAD_FEATURES).astype(jnp.float32)
        far_keys = pick_rows(key_head, offset)
        far_values = pick_rows(value_head, offset)
        delta = lax.optimization_barrier(jnp.sum(attended_head.astype(jnp.float32) * grad_head.astype(jnp.float32), -1)).reshape(blocks, SEGMENT)
        nearby_product = jnp.einsum('vlr,vwr->vlw', gradient_tiles, value_tiles)
        far_dot = jnp.dot(grad_head, far_values.T, preferred_element_type=jnp.float32).reshape(blocks, SEGMENT, SELECTED)
        nearby_gradient_slope = (nearby_weight * (nearby_product - delta[..., None])).astype(jnp.bfloat16)
        far_slope = (far_weight * (far_dot - delta[..., None])).astype(jnp.bfloat16).reshape(SEQUENCE_TOKENS, SELECTED)
        nearby_rounded = nearby_weight.astype(jnp.bfloat16).astype(jnp.float32)
        far_round = far_weight.astype(jnp.bfloat16).reshape(SEQUENCE_TOKENS, SELECTED)
        query_portion = jnp.einsum('xen,xna->xea', nearby_gradient_slope.astype(jnp.float32), key_tiles).reshape(SEQUENCE_TOKENS, HEAD_FEATURES)
        query_portion = query_portion + jnp.dot(far_slope, far_keys, preferred_element_type=jnp.float32)
        nearby_key = jnp.einsum('nsa,nsx->nax', nearby_gradient_slope.astype(jnp.float32), query_tiles).reshape(SEQUENCE_TOKENS, HEAD_FEATURES)
        nearby_value = jnp.einsum('nsa,nsx->nax', nearby_rounded, gradient_tiles).reshape(SEQUENCE_TOKENS, HEAD_FEATURES)
        far_key = jnp.dot(far_slope.T, query_head, preferred_element_type=jnp.float32)
        far_value = jnp.dot(far_round.T, grad_head, preferred_element_type=jnp.float32)
        place = (jnp.arange(DILATION, dtype=jnp.int32) == offset).astype(jnp.float32)

        def spread(near_rows, far_rows):
            return near_rows + (far_rows[:, None, :] * place[None, :, None]).reshape(SEQUENCE_TOKENS, HEAD_FEATURES)
        return ((query_portion * logit_scale).astype(jnp.bfloat16), (spread(nearby_key, far_key) * logit_scale).astype(jnp.bfloat16), spread(nearby_value, far_value).astype(jnp.bfloat16))
    query_grad, key_grad, value_grad = lax.map(backward_head, (split(queries), split(keys), split(values), split(attended), split(att_grad), head_ids))
    return (output, merge(query_grad), merge(key_grad), merge(value_grad))
```

```python
import functools
import math

import jax
import jax.numpy as jnp
from jax import lax
from jax.experimental import pallas as pl
from jax.experimental.pallas import tpu as pltpu
from jax.sharding import PartitionSpec as P

HEAD_FEATURES = 128
DILATION = 32
EPS = 1e-05
HIDDEN = -1e30
MESH = pl.DeviceIdType.MESH
F32 = jnp.float32
BF16 = jnp.bfloat16


def dot(a, b, left=1, right=0):
    return lax.dot_general(a, b, (((left,), (right,)), ((), ())), preferred_element_type=F32)


def iota(shape, dim):
    return lax.broadcasted_iota(jnp.int32, shape, dim)


def kernel(
    ctx_size, head_size, reach, group_heads,
    q_ref, k_ref, v_ref, og_ref, gain_ref, len_ref, level_ref,
    out_ref, dq_ref, dk_ref, dv_ref,
    far_ref, term_ref, back_ref, stat_ref, stats_ref,
    bias_ref, p_ref, pf_ref, ds_ref, sc_ref, o_ref, dqf_ref, own_ref, dkn_ref, dvn_ref,
    far_send, far_recv, back_send, back_recv, stat_send, stat_recv,
):
    toks, width = q_ref.shape
    heads = width // HEAD_FEATURES
    picked = toks // DILATION
    slots = reach + 1
    far_rows = slots * picked
    half = toks // 2
    full = width * head_size
    scale = HEAD_FEATURES ** (-0.5)
    scale2 = scale * math.log2(math.e)
    c = lax.axis_index("ctx")
    hp = lax.axis_index("head")

    def cols(h):
        return slice(h * HEAD_FEATURES, (h + 1) * HEAD_FEATURES)

    def wide_cols(h):
        return slice(width + h * HEAD_FEATURES, width + (h + 1) * HEAD_FEATURES)

    blocks = [(b * half, (b + 1) * half) for b in range(2)]

    for d in range(1, slots):
        @pl.when(c < d)
        def _():
            far_ref[d] = jnp.zeros(far_ref.shape[1:], BF16)

        @pl.when(c + d >= ctx_size)
        def _():
            back_ref[d - 1] = jnp.zeros(back_ref.shape[1:], BF16)

    barrier = pltpu.get_barrier_semaphore()
    for d in range(1, slots):
        @pl.when(c + d < ctx_size)
        def _():
            pl.semaphore_signal(barrier, inc=1, device_id=(c + d, hp), device_id_type=MESH)

        @pl.when(c >= d)
        def _():
            pl.semaphore_signal(barrier, inc=1, device_id=(c - d, hp), device_id_type=MESH)
    for e in range(1, head_size):
        peer = lax.rem(hp + e, head_size)
        pl.semaphore_signal(barrier, inc=1, device_id=(c, peer), device_id_type=MESH)

    def offset_of(h):
        return lax.rem(hp * heads + h, DILATION)

    row_of = iota((picked, toks), 0) * DILATION
    place_in = iota((picked, toks), 1)
    for h in range(heads):
        pick = jnp.where(place_in == row_of + offset_of(h), 1.0, 0.0).astype(BF16)
        far_ref[0, :, cols(h)] = dot(pick, k_ref[:, cols(h)]).astype(BF16)
        far_ref[0, :, wide_cols(h)] = dot(pick, v_ref[:, cols(h)]).astype(BF16)

    before = jnp.minimum(c, reach)
    after = jnp.minimum(ctx_size - 1 - c, reach)
    pl.semaphore_wait(barrier, before + after + (head_size - 1))

    def far_copy(d):
        return pltpu.make_async_remote_copy(
            src_ref=far_ref.at[0], dst_ref=far_ref.at[d],
            send_sem=far_send.at[d - 1], recv_sem=far_recv.at[d - 1],
            device_id=(c + d, hp), device_id_type=MESH,
        )

    def back_copy(d):
        return pltpu.make_async_remote_copy(
            src_ref=term_ref.at[d - 1], dst_ref=back_ref.at[d - 1],
            send_sem=back_send.at[d - 1], recv_sem=back_recv.at[d - 1],
            device_id=(c - d, hp), device_id_type=MESH,
        )

    def stat_copy(e):
        return pltpu.make_async_remote_copy(
            src_ref=stat_ref, dst_ref=stats_ref.at[e - 1],
            send_sem=stat_send.at[e - 1], recv_sem=stat_recv.at[e - 1],
            device_id=(c, lax.rem(hp + e, head_size)), device_id_type=MESH,
        )

    for d in range(1, slots):
        @pl.when(c + d < ctx_size)
        def _():
            far_copy(d).start()

    place_q = iota((1, toks), 1) + c * toks
    first = jnp.zeros((1, toks), jnp.int32)
    end = jnp.int32(0)
    for i in range(len_ref.shape[0]):
        end = end + len_ref[i]
        first = jnp.maximum(first, jnp.where(place_q >= end, end, 0))
    for low, high in blocks:
        place_k = iota((high, half), 0) + c * toks
        seen = (place_k <= place_q[:, low:high]) & (place_k >= first[:, low:high])
        bias_ref[0:high, low:high] = jnp.where(seen, 0.0, HIDDEN)

    tops, sums = [], []
    for h in range(heads):
        values_t = v_ref[:, cols(h)].T
        top_parts, sum_parts = [], []
        for low, high in blocks:
            logit = dot(k_ref[0:high, cols(h)], q_ref[low:high, cols(h)], 1, 1)
            logit = logit * scale2 + bias_ref[0:high, low:high]
            top = jnp.max(logit, axis=0, keepdims=True)
            weight = jnp.exp2(logit - top)
            top_parts.append(top)
            sum_parts.append(jnp.sum(weight, axis=0, keepdims=True))
            weight = weight.astype(BF16)
            p_ref[h, 0:high, low:high] = weight
            o_ref[h, :, low:high] = dot(values_t[:, 0:high], weight)
        tops.append(jnp.concatenate(top_parts, axis=1))
        sums.append(jnp.concatenate(sum_parts, axis=1))
        scaled = og_ref[:, cols(h)].astype(F32) * gain_ref[:, cols(h)]
        sc_ref[h] = scaled.T

    for d in range(1, slots):
        @pl.when(c >= d)
        def _():
            far_copy(d).wait_recv()

    row = iota((far_rows, toks), 0)
    counter = (c - row // picked) * picked + row % picked
    near_scale, far_scale = [], []
    stats = [jnp.zeros((1, toks), F32) for _ in range(4)]
    for h in range(heads):
        far_k = far_ref[:, :, cols(h)].reshape(far_rows, HEAD_FEATURES)
        far_v = far_ref[:, :, wide_cols(h)].reshape(far_rows, HEAD_FEATURES)
        level = level_ref[(hp * heads + h) // group_heads]
        skip = jnp.left_shift(jnp.int32(1), level) - 1
        place_k = counter * DILATION + offset_of(h)
        seen = (place_k <= place_q) & (place_k >= first) & ((counter & skip) == 0)
        logit = jnp.where(seen, dot(far_k, q_ref[:, cols(h)], 1, 1) * scale2, HIDDEN)
        top = jnp.maximum(tops[h], jnp.max(logit, axis=0, keepdims=True))
        weight = jnp.exp2(logit - top)
        shrink = jnp.exp2(tops[h] - top)
        inverse = 1.0 / (sums[h] * shrink + jnp.sum(weight, axis=0, keepdims=True))
        weight = weight.astype(BF16)
        pf_ref[h] = weight
        near_scale.append(shrink * inverse)
        far_scale.append(inverse)
        attended = (o_ref[h] * near_scale[h] + dot(far_v, weight, 0, 0) * inverse).astype(BF16)
        attended = attended.astype(F32)
        o_ref[h] = attended
        scaled = sc_ref[h]
        terms = (attended, attended * attended, scaled, scaled * attended)
        stats = [s + jnp.sum(t, axis=0, keepdims=True) for s, t in zip(stats, terms)]

    for i in range(4):
        stat_ref[i : i + 1, :] = stats[i]
    stat_ref[4:8, :] = jnp.zeros((4, toks), F32)
    for e in range(1, head_size):
        stat_copy(e).start()
    for e in range(1, head_size):
        stat_copy(e).wait_recv()
    total = stat_ref[...]
    for e in range(1, head_size):
        total = total + stats_ref[e - 1]
    total = total / full
    mean, square, grad_mean, cross = (total[i : i + 1, :] for i in range(4))
    rstd = lax.rsqrt(square - mean * mean + EPS)
    shift = -mean * rstd
    proj = rstd * (cross - mean * grad_mean)

    for h in range(heads):
        attended = o_ref[h]
        normed = attended * rstd + shift
        out_ref[:, cols(h)] = (normed.T * gain_ref[:, cols(h)]).astype(BF16)
        grad = rstd * (sc_ref[h] - grad_mean - normed * proj)
        sc_ref[h] = grad
        grad = (grad * far_scale[h]).astype(BF16)
        delta = jnp.sum(grad.astype(F32) * attended, axis=0, keepdims=True)
        far_k = far_ref[:, :, cols(h)].reshape(far_rows, HEAD_FEATURES)
        far_v = far_ref[:, :, wide_cols(h)].reshape(far_rows, HEAD_FEATURES)
        weight = pf_ref[h]
        slope = (weight.astype(F32) * (dot(far_v, grad) - delta)).astype(BF16)
        dqf_ref[h] = dot(far_k, slope, 0, 0)
        key_term = dot(slope, q_ref[:, cols(h)]) * scale
        value_term = dot(weight, grad, 1, 1)
        own_ref[:, cols(h)] = key_term[0:picked]
        own_ref[:, wide_cols(h)] = value_term[0:picked]
        term_ref[:, :, cols(h)] = (
            key_term[picked:].astype(BF16).reshape(reach, picked, HEAD_FEATURES)
        )
        term_ref[:, :, wide_cols(h)] = (
            value_term[picked:].astype(BF16).reshape(reach, picked, HEAD_FEATURES)
        )

    for d in range(1, slots):
        @pl.when(c >= d)
        def _():
            back_copy(d).start()

    for h in range(heads):
        grad = (sc_ref[h] * near_scale[h]).astype(BF16)
        delta = jnp.sum(grad.astype(F32) * o_ref[h], axis=0, keepdims=True)
        keys_t = k_ref[:, cols(h)].T
        for low, high in blocks:
            product = dot(v_ref[0:high, cols(h)], grad[:, low:high])
            weight = p_ref[h, 0:high, low:high].astype(F32)
            slope = (weight * (product - delta[:, low:high])).astype(BF16)
            ds_ref[0:high, low:high] = slope
            query_grad = dot(keys_t[:, 0:high], slope) + dqf_ref[h, :, low:high]
            dq_ref[low:high, cols(h)] = (query_grad * scale).T.astype(BF16)
        for low, high in blocks:
            dkn_ref[low:high, cols(h)] = (
                dot(ds_ref[low:high, low:toks], q_ref[low:toks, cols(h)]) * scale
            )
            dvn_ref[low:high, cols(h)] = dot(p_ref[h, low:high, low:toks], grad[:, low:toks], 1, 1)

    for d in range(1, slots):
        @pl.when(c + d < ctx_size)
        def _():
            back_copy(d).wait_recv()
    mine = own_ref[...]
    for d in range(1, slots):
        mine = mine + back_ref[d - 1].astype(F32)
    upper = mine.astype(BF16)
    lower = (mine - upper.astype(F32)).astype(BF16)
    both = jnp.concatenate([upper, lower], axis=0)
    spot = iota((toks, 2 * picked), 0)
    target = iota((toks, 2 * picked), 1) % picked * DILATION
    for h in range(heads):
        place = jnp.where(spot == target + offset_of(h), 1.0, 0.0).astype(BF16)
        dk_ref[:, cols(h)] = (dkn_ref[:, cols(h)] + dot(place, both[:, cols(h)])).astype(BF16)
        dv_ref[:, cols(h)] = (dvn_ref[:, cols(h)] + dot(place, both[:, wide_cols(h)])).astype(BF16)

    for d in range(1, slots):
        @pl.when(c + d < ctx_size)
        def _():
            far_copy(d).wait_send()

        @pl.when(c >= d)
        def _():
            back_copy(d).wait_send()
    for e in range(1, head_size):
        stat_copy(e).wait_send()


def shards(queries, keys, values, out_grad, norm_gain, doc_lengths, group_level):
    toks, width = queries.shape
    heads = width // HEAD_FEATURES
    ctx_size, head_size = lax.axis_size("ctx"), lax.axis_size("head")
    group_heads = heads * head_size // group_level.shape[0]
    picked = toks // DILATION
    reach = max(ctx_size // 2, 1)
    slots = reach + 1
    vmem = pl.BlockSpec(memory_space=pltpu.VMEM)
    smem = pl.BlockSpec(memory_space=pltpu.SMEM)
    grads = jax.ShapeDtypeStruct((toks, width), BF16)
    return pl.pallas_call(
        functools.partial(kernel, ctx_size, head_size, reach, group_heads),
        out_shape=(grads,) * 4,
        in_specs=[vmem] * 5 + [smem] * 2,
        out_specs=(vmem,) * 4,
        scratch_shapes=[
            pltpu.VMEM((slots, picked, 2 * width), BF16),
            pltpu.VMEM((reach, picked, 2 * width), BF16),
            pltpu.VMEM((reach, picked, 2 * width), BF16),
            pltpu.VMEM((8, toks), F32),
            pltpu.VMEM((head_size - 1, 8, toks), F32),
            pltpu.VMEM((toks, toks), F32),
            pltpu.VMEM((heads, toks, toks), BF16),
            pltpu.VMEM((heads, slots * picked, toks), BF16),
            pltpu.VMEM((toks, toks), BF16),
            pltpu.VMEM((heads, HEAD_FEATURES, toks), F32),
            pltpu.VMEM((heads, HEAD_FEATURES, toks), F32),
            pltpu.VMEM((heads, HEAD_FEATURES, toks), F32),
            pltpu.VMEM((picked, 2 * width), F32),
            pltpu.VMEM((toks, width), F32),
            pltpu.VMEM((toks, width), F32),
            pltpu.SemaphoreType.DMA((reach,)),
            pltpu.SemaphoreType.DMA((reach,)),
            pltpu.SemaphoreType.DMA((reach,)),
            pltpu.SemaphoreType.DMA((reach,)),
            pltpu.SemaphoreType.DMA((head_size - 1,)),
            pltpu.SemaphoreType.DMA((head_size - 1,)),
        ],
        compiler_params=pltpu.CompilerParams(
            collective_id=0, has_side_effects=True, vmem_limit_bytes=48 * 1024 * 1024
        ),
    )(queries, keys, values, out_grad, norm_gain.reshape(1, width), doc_lengths, group_level)


def solution(mesh):
    split = P("ctx", "head")
    return jax.shard_map(
        shards,
        mesh=mesh,
        in_specs=(split, split, split, split, P("head"), P(), P()),
        out_specs=(split, split, split, split),
        check_vma=False,
    )
```

```python
import functools
import math

import jax
import jax.numpy as jnp
from jax import lax
from jax.experimental import pallas as pl
from jax.experimental.pallas import tpu as pltpu
from jax.sharding import PartitionSpec as P

HEAD_FEATURES = 128
DILATION = 32
EPS = 1e-05
HIDDEN = -1e30
MESH = pl.DeviceIdType.MESH
F32 = jnp.float32
BF16 = jnp.bfloat16


def dot(a, b, left=1, right=0):
    return lax.dot_general(a, b, (((left,), (right,)), ((), ())), preferred_element_type=F32)


def iota(shape, dim):
    return lax.broadcasted_iota(jnp.int32, shape, dim)


def kernel(
    ctx_size, head_size, reach, group_heads,
    q_hbm, k_hbm, v_hbm, og_hbm, gain_hbm, len_hbm, level_hbm,
    out_ref, dq_ref, dk_ref, dv_ref,
    far_ref, term_ref, back_ref, stat_ref, stats_ref,
    q_ref, k_ref, v_ref, og_ref, gain_ref, len_ref, level_ref, load_sem,
    bias_ref, p_ref, pf_ref, ds_ref, sc_ref, o_ref, dqf_ref, own_ref, dkn_ref, dvn_ref,
    far_send, far_recv, back_send, back_recv, stat_send, stat_recv,
):
    loads = [
        pltpu.make_async_copy(source, target, load_sem.at[i])
        for i, (source, target) in enumerate(
            (
                (k_hbm, k_ref), (v_hbm, v_ref), (len_hbm, len_ref), (level_hbm, level_ref),
                (q_hbm, q_ref), (gain_hbm, gain_ref), (og_hbm, og_ref),
            )
        )
    ]
    for load in loads:
        load.start()
    toks, width = q_ref.shape
    heads = width // HEAD_FEATURES
    picked = toks // DILATION
    slots = reach + 1
    far_rows = slots * picked
    half = toks // 2
    full = width * head_size
    scale = HEAD_FEATURES ** (-0.5)
    scale2 = scale * math.log2(math.e)
    c = lax.axis_index("ctx")
    hp = lax.axis_index("head")

    def cols(h):
        return slice(h * HEAD_FEATURES, (h + 1) * HEAD_FEATURES)

    def wide_cols(h):
        return slice(width + h * HEAD_FEATURES, width + (h + 1) * HEAD_FEATURES)

    halves = back_ref.shape[0]
    part_heads = heads // halves

    blocks = [(b * half, (b + 1) * half) for b in range(2)]

    barrier = pltpu.get_barrier_semaphore()
    for d in range(1, slots):
        @pl.when(c + d < ctx_size)
        def _():
            pl.semaphore_signal(barrier, inc=1, device_id=(c + d, hp), device_id_type=MESH)

        @pl.when(c >= d)
        def _():
            pl.semaphore_signal(barrier, inc=1, device_id=(c - d, hp), device_id_type=MESH)
    for e in range(1, head_size):
        peer = lax.rem(hp + e, head_size)
        pl.semaphore_signal(barrier, inc=1, device_id=(c, peer), device_id_type=MESH)

    for d in range(1, slots):
        @pl.when(c < d)
        def _():
            far_ref[d] = jnp.zeros(far_ref.shape[1:], BF16)

        @pl.when(c + d >= ctx_size)
        def _():
            back_ref[:, d - 1] = jnp.zeros((halves,) + back_ref.shape[2:], BF16)

    loads[0].wait()
    loads[1].wait()

    def offset_of(h):
        return lax.rem(hp * heads + h, DILATION)

    row_of = iota((picked, toks), 0) * DILATION
    place_in = iota((picked, toks), 1)
    for h in range(heads):
        pick = jnp.where(place_in == row_of + offset_of(h), 1.0, 0.0).astype(BF16)
        far_ref[0, :, cols(h)] = dot(pick, k_ref[:, cols(h)]).astype(BF16)
        far_ref[0, :, wide_cols(h)] = dot(pick, v_ref[:, cols(h)]).astype(BF16)

    before = jnp.minimum(c, reach)
    after = jnp.minimum(ctx_size - 1 - c, reach)
    pl.semaphore_wait(barrier, before + after + (head_size - 1))

    def far_copy(d):
        return pltpu.make_async_remote_copy(
            src_ref=far_ref.at[0], dst_ref=far_ref.at[d],
            send_sem=far_send.at[d - 1], recv_sem=far_recv.at[d - 1],
            device_id=(c + d, hp), device_id_type=MESH,
        )

    def back_copy(part, d):
        return pltpu.make_async_remote_copy(
            src_ref=term_ref.at[part, d - 1], dst_ref=back_ref.at[part, d - 1],
            send_sem=back_send.at[part, d - 1], recv_sem=back_recv.at[part, d - 1],
            device_id=(c - d, hp), device_id_type=MESH,
        )

    def stat_copy(e):
        return pltpu.make_async_remote_copy(
            src_ref=stat_ref, dst_ref=stats_ref.at[e - 1],
            send_sem=stat_send.at[e - 1], recv_sem=stat_recv.at[e - 1],
            device_id=(c, lax.rem(hp + e, head_size)), device_id_type=MESH,
        )

    for d in range(1, slots):
        @pl.when(c + d < ctx_size)
        def _():
            far_copy(d).start()

    for load in loads[2:]:
        load.wait()

    place_q = iota((1, toks), 1) + c * toks
    first = jnp.zeros((1, toks), jnp.int32)
    end = jnp.int32(0)
    for i in range(len_ref.shape[0]):
        end = end + len_ref[i]
        first = jnp.maximum(first, jnp.where(place_q >= end, end, 0))
    for low, high in blocks:
        place_k = iota((high, half), 0) + c * toks
        seen = (place_k <= place_q[:, low:high]) & (place_k >= first[:, low:high])
        bias_ref[0:high, low:high] = jnp.where(seen, 0.0, HIDDEN)

    tops, sums = [], []
    for h in range(heads):
        values_t = v_ref[:, cols(h)].T
        top_parts, sum_parts = [], []
        for low, high in blocks:
            logit = dot(k_ref[0:high, cols(h)], q_ref[low:high, cols(h)], 1, 1)
            logit = logit * scale2 + bias_ref[0:high, low:high]
            top = jnp.max(logit, axis=0, keepdims=True)
            weight = jnp.exp2(logit - top)
            top_parts.append(top)
            sum_parts.append(jnp.sum(weight, axis=0, keepdims=True))
            weight = weight.astype(BF16)
            p_ref[h, 0:high, low:high] = weight
            o_ref[h, :, low:high] = dot(values_t[:, 0:high], weight)
        tops.append(jnp.concatenate(top_parts, axis=1))
        sums.append(jnp.concatenate(sum_parts, axis=1))
        scaled = og_ref[:, cols(h)].astype(F32) * gain_ref[:, cols(h)]
        sc_ref[h] = scaled.T

    for d in range(1, slots):
        @pl.when(c >= d)
        def _():
            far_copy(d).wait_recv()

    row = iota((far_rows, toks), 0)
    counter = (c - row // picked) * picked + row % picked
    near_scale, far_scale = [], []
    stats = [jnp.zeros((1, toks), F32) for _ in range(4)]
    for h in range(heads):
        far_k = far_ref[:, :, cols(h)].reshape(far_rows, HEAD_FEATURES)
        far_v = far_ref[:, :, wide_cols(h)].reshape(far_rows, HEAD_FEATURES)
        level = level_ref[(hp * heads + h) // group_heads]
        skip = jnp.left_shift(jnp.int32(1), level) - 1
        place_k = counter * DILATION + offset_of(h)
        seen = (place_k <= place_q) & (place_k >= first) & ((counter & skip) == 0)
        logit = jnp.where(seen, dot(far_k, q_ref[:, cols(h)], 1, 1) * scale2, HIDDEN)
        top = jnp.maximum(tops[h], jnp.max(logit, axis=0, keepdims=True))
        weight = jnp.exp2(logit - top)
        shrink = jnp.exp2(tops[h] - top)
        inverse = 1.0 / (sums[h] * shrink + jnp.sum(weight, axis=0, keepdims=True))
        weight = weight.astype(BF16)
        pf_ref[h] = weight
        near_scale.append(shrink * inverse)
        far_scale.append(inverse)
        attended = (o_ref[h] * near_scale[h] + dot(far_v, weight, 0, 0) * inverse).astype(BF16)
        attended = attended.astype(F32)
        o_ref[h] = attended
        scaled = sc_ref[h]
        terms = (attended, attended * attended, scaled, scaled * attended)
        stats = [s + jnp.sum(t, axis=0, keepdims=True) for s, t in zip(stats, terms)]

    for i in range(4):
        stat_ref[i : i + 1, :] = stats[i]
    stat_ref[4:8, :] = jnp.zeros((4, toks), F32)
    for e in range(1, head_size):
        stat_copy(e).start()
    for e in range(1, head_size):
        stat_copy(e).wait_recv()
    total = stat_ref[...]
    for e in range(1, head_size):
        total = total + stats_ref[e - 1]
    total = total / full
    mean, square, grad_mean, cross = (total[i : i + 1, :] for i in range(4))
    rstd = lax.rsqrt(square - mean * mean + EPS)
    shift = -mean * rstd
    proj = rstd * (cross - mean * grad_mean)

    for h in range(heads):
        attended = o_ref[h]
        normed = attended * rstd + shift
        out_ref[:, cols(h)] = (normed.T * gain_ref[:, cols(h)]).astype(BF16)
        grad = rstd * (sc_ref[h] - grad_mean - normed * proj)
        sc_ref[h] = grad
        grad = (grad * far_scale[h]).astype(BF16)
        delta = jnp.sum(grad.astype(F32) * attended, axis=0, keepdims=True)
        far_k = far_ref[:, :, cols(h)].reshape(far_rows, HEAD_FEATURES)
        far_v = far_ref[:, :, wide_cols(h)].reshape(far_rows, HEAD_FEATURES)
        weight = pf_ref[h]
        slope = (weight.astype(F32) * (dot(far_v, grad) - delta)).astype(BF16)
        dqf_ref[h] = dot(far_k, slope, 0, 0)
        key_term = dot(slope, q_ref[:, cols(h)]) * scale
        value_term = dot(weight, grad, 1, 1)
        own_ref[:, cols(h)] = key_term[0:picked]
        own_ref[:, wide_cols(h)] = value_term[0:picked]
        part, spot = divmod(h, part_heads)
        term_ref[part, :, :, cols(spot)] = (
            key_term[picked:].astype(BF16).reshape(reach, picked, HEAD_FEATURES)
        )
        term_ref[part, :, :, cols(spot + part_heads)] = (
            value_term[picked:].astype(BF16).reshape(reach, picked, HEAD_FEATURES)
        )
        if spot == part_heads - 1:
            for d in reversed(range(1, slots)):
                @pl.when(c >= d)
                def _():
                    back_copy(part, d).start()

    for h in range(heads):
        grad = (sc_ref[h] * near_scale[h]).astype(BF16)
        delta = jnp.sum(grad.astype(F32) * o_ref[h], axis=0, keepdims=True)
        keys_t = k_ref[:, cols(h)].T
        for low, high in blocks:
            product = dot(v_ref[0:high, cols(h)], grad[:, low:high])
            weight = p_ref[h, 0:high, low:high].astype(F32)
            slope = (weight * (product - delta[:, low:high])).astype(BF16)
            ds_ref[0:high, low:high] = slope
            query_grad = dot(keys_t[:, 0:high], slope) + dqf_ref[h, :, low:high]
            dq_ref[low:high, cols(h)] = (query_grad * scale).T.astype(BF16)
        for low, high in blocks:
            dkn_ref[low:high, cols(h)] = (
                dot(ds_ref[low:high, low:toks], q_ref[low:toks, cols(h)]) * scale
            )
            dvn_ref[low:high, cols(h)] = dot(p_ref[h, low:high, low:toks], grad[:, low:toks], 1, 1)

    spot = iota((toks, 2 * picked), 0)
    target = iota((toks, 2 * picked), 1) % picked * DILATION
    for part in range(halves):
        for d in range(1, slots):
            @pl.when(c + d < ctx_size)
            def _():
                back_copy(part, d).wait_recv()
        theirs = back_ref[part, 0].astype(F32)
        for d in range(2, slots):
            theirs = theirs + back_ref[part, d - 1].astype(F32)
        for inner in range(part_heads):
            h = part * part_heads + inner
            place = jnp.where(spot == target + offset_of(h), 1.0, 0.0).astype(BF16)
            for near, out, own, column in (
                (dkn_ref, dk_ref, cols(h), inner),
                (dvn_ref, dv_ref, wide_cols(h), inner + part_heads),
            ):
                mine = own_ref[:, own] + theirs[:, cols(column)]
                upper = mine.astype(BF16)
                lower = (mine - upper.astype(F32)).astype(BF16)
                both = jnp.concatenate([upper, lower], axis=0)
                out[:, cols(h)] = (near[:, cols(h)] + dot(place, both)).astype(BF16)

    for d in range(1, slots):
        @pl.when(c + d < ctx_size)
        def _():
            far_copy(d).wait_send()

        @pl.when(c >= d)
        def _():
            for part in range(halves):
                back_copy(part, d).wait_send()
    for e in range(1, head_size):
        stat_copy(e).wait_send()


def store(*refs):
    count = len(refs) // 2
    sems = refs[-1]
    copies = [
        pltpu.make_async_copy(refs[i], refs[count + i], sems.at[i]) for i in range(count)
    ]
    for copy in copies:
        copy.start()
    for copy in copies:
        copy.wait()


def shards(queries, keys, values, out_grad, norm_gain, doc_lengths, group_level):
    toks, width = queries.shape
    heads = width // HEAD_FEATURES
    ctx_size, head_size = lax.axis_size("ctx"), lax.axis_size("head")
    group_heads = heads * head_size // group_level.shape[0]
    picked = toks // DILATION
    reach = max(ctx_size // 2, 1)
    slots = reach + 1
    vmem = pl.BlockSpec(memory_space=pltpu.VMEM)
    hbm = pl.BlockSpec(memory_space=pltpu.HBM)
    halves = 2 if heads % 2 == 0 else 1
    grads = jax.ShapeDtypeStruct((toks, width), BF16)
    gain = norm_gain.reshape(1, width)
    operands = (queries, keys, values, out_grad, gain, doc_lengths, group_level)
    results = pl.pallas_call(
        functools.partial(kernel, ctx_size, head_size, reach, group_heads),
        out_shape=(grads,) * 4,
        in_specs=[hbm] * 7,
        out_specs=(vmem,) * 4,
        scratch_shapes=[
            pltpu.VMEM((slots, picked, 2 * width), BF16),
            pltpu.VMEM((halves, reach, picked, 2 * width // halves), BF16),
            pltpu.VMEM((halves, reach, picked, 2 * width // halves), BF16),
            pltpu.VMEM((8, toks), F32),
            pltpu.VMEM((head_size - 1, 8, toks), F32),
            pltpu.VMEM((toks, width), BF16),
            pltpu.VMEM((toks, width), BF16),
            pltpu.VMEM((toks, width), BF16),
            pltpu.VMEM((toks, width), BF16),
            pltpu.VMEM((1, width), F32),
            pltpu.SMEM(doc_lengths.shape, jnp.int32),
            pltpu.SMEM(group_level.shape, jnp.int32),
            pltpu.SemaphoreType.DMA((7,)),
            pltpu.VMEM((toks, toks), F32),
            pltpu.VMEM((heads, toks, toks), BF16),
            pltpu.VMEM((heads, slots * picked, toks), BF16),
            pltpu.VMEM((toks, toks), BF16),
            pltpu.VMEM((heads, HEAD_FEATURES, toks), F32),
            pltpu.VMEM((heads, HEAD_FEATURES, toks), F32),
            pltpu.VMEM((heads, HEAD_FEATURES, toks), F32),
            pltpu.VMEM((picked, 2 * width), F32),
            pltpu.VMEM((toks, width), F32),
            pltpu.VMEM((toks, width), F32),
            pltpu.SemaphoreType.DMA((reach,)),
            pltpu.SemaphoreType.DMA((reach,)),
            pltpu.SemaphoreType.DMA((halves, reach)),
            pltpu.SemaphoreType.DMA((halves, reach)),
            pltpu.SemaphoreType.DMA((head_size - 1,)),
            pltpu.SemaphoreType.DMA((head_size - 1,)),
        ],
        compiler_params=pltpu.CompilerParams(
            collective_id=0, has_side_effects=True, vmem_limit_bytes=48 * 1024 * 1024
        ),
    )(*(pltpu.with_memory_space_constraint(given, pltpu.HBM) for given in operands))
    return pl.pallas_call(
        store,
        out_shape=(grads,) * 4,
        in_specs=[vmem] * 4,
        out_specs=(hbm,) * 4,
        scratch_shapes=[pltpu.SemaphoreType.DMA((4,))],
    )(*results)


def solution(mesh):
    split = P("ctx", "head")
    return jax.shard_map(
        shards,
        mesh=mesh,
        in_specs=(split, split, split, split, P("head"), P(), P()),
        out_specs=(split, split, split, split),
        check_vma=False,
    )
```

```python
import functools
import math

import jax
import jax.numpy as jnp
from jax import lax
from jax.experimental import pallas as pl
from jax.experimental.pallas import tpu as pltpu
from jax.sharding import PartitionSpec as P

HEAD_FEATURES = 128
DILATION = 32
EPS = 1e-05
HIDDEN = -1e30
MESH = pl.DeviceIdType.MESH
F32 = jnp.float32
BF16 = jnp.bfloat16


def dot(a, b, left=1, right=0):
    return lax.dot_general(a, b, (((left,), (right,)), ((), ())), preferred_element_type=F32)


def iota(shape, dim):
    return lax.broadcasted_iota(jnp.int32, shape, dim)


def cols(h):
    return slice(h * HEAD_FEATURES, (h + 1) * HEAD_FEATURES)


def blocks_of(toks):
    return [(0, toks // 2), (toks // 2, toks)]


def near_backward(h, q_ref, k_ref, v_ref, p_ref, ds_ref, sc_ref, o_ref, dqf_ref, near_ref, dq_ref):
    toks = q_ref.shape[0]
    blocks = blocks_of(toks)
    scale = HEAD_FEATURES ** (-0.5)
    grad = (sc_ref[h] * near_ref[h]).astype(BF16)
    delta = jnp.sum(grad.astype(F32) * o_ref[h], axis=0, keepdims=True)
    keys_t = k_ref[:, cols(h)].T
    for low, high in blocks:
        product = dot(v_ref[0:high, cols(h)], grad[:, low:high])
        weight = p_ref[h, 0:high, low:high].astype(F32)
        slope = (weight * (product - delta[:, low:high])).astype(BF16)
        ds_ref[0:high, low:high] = slope
        query_grad = dot(keys_t[:, 0:high], slope) + dqf_ref[h, :, low:high]
        dq_ref[low:high, cols(h)] = (query_grad * scale).T.astype(BF16)
    return [
        (
            low,
            high,
            dot(ds_ref[low:high, low:toks], q_ref[low:toks, cols(h)]) * scale,
            dot(p_ref[h, low:high, low:toks], grad[:, low:toks], 1, 1),
        )
        for low, high in blocks
    ]


def kernel(
    ctx_size, head_size, reach, group_heads,
    q_hbm, k_hbm, v_hbm, og_hbm, gain_hbm, len_hbm, level_hbm,
    out_ref, dq_ref, dkn_ref, dvn_ref, own_ref,
    q_ref, k_ref, v_ref, p_ref, sc_ref, o_ref, dqf_ref, near_ref,
    far_ref, term_ref, back_ref, stat_ref, stats_ref,
    og_ref, gain_ref, len_ref, level_ref, load_sem,
    bias_ref, pf_ref, ds_ref,
    far_send, far_recv, back_send, back_recv, stat_send, stat_recv,
):
    loads = [
        pltpu.make_async_copy(source, target, load_sem.at[i])
        for i, (source, target) in enumerate(
            (
                (k_hbm, k_ref), (v_hbm, v_ref), (len_hbm, len_ref), (level_hbm, level_ref),
                (q_hbm, q_ref), (gain_hbm, gain_ref), (og_hbm, og_ref),
            )
        )
    ]
    for load in loads:
        load.start()
    toks, width = q_ref.shape
    heads = width // HEAD_FEATURES
    picked = toks // DILATION
    slots = reach + 1
    far_rows = slots * picked
    half = toks // 2
    early = dkn_ref.shape[1] // HEAD_FEATURES
    full = width * head_size
    scale = HEAD_FEATURES ** (-0.5)
    scale2 = scale * math.log2(math.e)
    c = lax.axis_index("ctx")
    hp = lax.axis_index("head")

    def wide_cols(h):
        return slice(width + h * HEAD_FEATURES, width + (h + 1) * HEAD_FEATURES)

    halves = back_ref.shape[0]
    part_heads = heads // halves

    blocks = blocks_of(toks)

    barrier = pltpu.get_barrier_semaphore()
    for d in range(1, slots):
        @pl.when(c + d < ctx_size)
        def _():
            pl.semaphore_signal(barrier, inc=1, device_id=(c + d, hp), device_id_type=MESH)

        @pl.when(c >= d)
        def _():
            pl.semaphore_signal(barrier, inc=1, device_id=(c - d, hp), device_id_type=MESH)
    for e in range(1, head_size):
        peer = lax.rem(hp + e, head_size)
        pl.semaphore_signal(barrier, inc=1, device_id=(c, peer), device_id_type=MESH)

    for d in range(1, slots):
        @pl.when(c < d)
        def _():
            far_ref[d] = jnp.zeros(far_ref.shape[1:], BF16)

        @pl.when(c + d >= ctx_size)
        def _():
            back_ref[:, d - 1] = jnp.zeros((halves,) + back_ref.shape[2:], BF16)

    loads[0].wait()
    loads[1].wait()

    def offset_of(h):
        return lax.rem(hp * heads + h, DILATION)

    row_of = iota((picked, toks), 0) * DILATION
    place_in = iota((picked, toks), 1)
    for h in range(heads):
        pick = jnp.where(place_in == row_of + offset_of(h), 1.0, 0.0).astype(BF16)
        far_ref[0, :, cols(h)] = dot(pick, k_ref[:, cols(h)]).astype(BF16)
        far_ref[0, :, wide_cols(h)] = dot(pick, v_ref[:, cols(h)]).astype(BF16)

    before = jnp.minimum(c, reach)
    after = jnp.minimum(ctx_size - 1 - c, reach)
    pl.semaphore_wait(barrier, before + after + (head_size - 1))

    def far_copy(d):
        return pltpu.make_async_remote_copy(
            src_ref=far_ref.at[0], dst_ref=far_ref.at[d],
            send_sem=far_send.at[d - 1], recv_sem=far_recv.at[d - 1],
            device_id=(c + d, hp), device_id_type=MESH,
        )

    def back_copy(part, d):
        return pltpu.make_async_remote_copy(
            src_ref=term_ref.at[part, d - 1], dst_ref=back_ref.at[part, d - 1],
            send_sem=back_send.at[part, d - 1], recv_sem=back_recv.at[part, d - 1],
            device_id=(c - d, hp), device_id_type=MESH,
        )

    def stat_copy(e):
        return pltpu.make_async_remote_copy(
            src_ref=stat_ref, dst_ref=stats_ref.at[e - 1],
            send_sem=stat_send.at[e - 1], recv_sem=stat_recv.at[e - 1],
            device_id=(c, lax.rem(hp + e, head_size)), device_id_type=MESH,
        )

    for d in range(1, slots):
        @pl.when(c + d < ctx_size)
        def _():
            far_copy(d).start()

    for load in loads[2:]:
        load.wait()

    place_q = iota((1, toks), 1) + c * toks
    first = jnp.zeros((1, toks), jnp.int32)
    end = jnp.int32(0)
    for i in range(len_ref.shape[0]):
        end = end + len_ref[i]
        first = jnp.maximum(first, jnp.where(place_q >= end, end, 0))
    for low, high in blocks:
        place_k = iota((high, half), 0) + c * toks
        seen = (place_k <= place_q[:, low:high]) & (place_k >= first[:, low:high])
        bias_ref[0:high, low:high] = jnp.where(seen, 0.0, HIDDEN)

    tops, sums = [], []
    for h in range(heads):
        values_t = v_ref[:, cols(h)].T
        top_parts, sum_parts = [], []
        for low, high in blocks:
            logit = dot(k_ref[0:high, cols(h)], q_ref[low:high, cols(h)], 1, 1)
            logit = logit * scale2 + bias_ref[0:high, low:high]
            top = jnp.max(logit, axis=0, keepdims=True)
            weight = jnp.exp2(logit - top)
            top_parts.append(top)
            sum_parts.append(jnp.sum(weight, axis=0, keepdims=True))
            weight = weight.astype(BF16)
            p_ref[h, 0:high, low:high] = weight
            o_ref[h, :, low:high] = dot(values_t[:, 0:high], weight)
        tops.append(jnp.concatenate(top_parts, axis=1))
        sums.append(jnp.concatenate(sum_parts, axis=1))
        scaled = og_ref[:, cols(h)].astype(F32) * gain_ref[:, cols(h)]
        sc_ref[h] = scaled.T

    for d in range(1, slots):
        @pl.when(c >= d)
        def _():
            far_copy(d).wait_recv()

    row = iota((far_rows, toks), 0)
    counter = (c - row // picked) * picked + row % picked
    near_scale, far_scale = [], []
    stats = [jnp.zeros((1, toks), F32) for _ in range(4)]
    for h in range(heads):
        far_k = far_ref[:, :, cols(h)].reshape(far_rows, HEAD_FEATURES)
        far_v = far_ref[:, :, wide_cols(h)].reshape(far_rows, HEAD_FEATURES)
        level = level_ref[(hp * heads + h) // group_heads]
        skip = jnp.left_shift(jnp.int32(1), level) - 1
        place_k = counter * DILATION + offset_of(h)
        seen = (place_k <= place_q) & (place_k >= first) & ((counter & skip) == 0)
        logit = jnp.where(seen, dot(far_k, q_ref[:, cols(h)], 1, 1) * scale2, HIDDEN)
        top = jnp.maximum(tops[h], jnp.max(logit, axis=0, keepdims=True))
        weight = jnp.exp2(logit - top)
        shrink = jnp.exp2(tops[h] - top)
        inverse = 1.0 / (sums[h] * shrink + jnp.sum(weight, axis=0, keepdims=True))
        weight = weight.astype(BF16)
        pf_ref[h] = weight
        near_scale.append(shrink * inverse)
        near_ref[h] = near_scale[h]
        far_scale.append(inverse)
        attended = (o_ref[h] * near_scale[h] + dot(far_v, weight, 0, 0) * inverse).astype(BF16)
        attended = attended.astype(F32)
        o_ref[h] = attended
        scaled = sc_ref[h]
        terms = (attended, attended * attended, scaled, scaled * attended)
        stats = [s + jnp.sum(t, axis=0, keepdims=True) for s, t in zip(stats, terms)]

    for i in range(4):
        stat_ref[i : i + 1, :] = stats[i]
    stat_ref[4:8, :] = jnp.zeros((4, toks), F32)
    for e in range(1, head_size):
        stat_copy(e).start()
    for e in range(1, head_size):
        stat_copy(e).wait_recv()
    total = stat_ref[...]
    for e in range(1, head_size):
        total = total + stats_ref[e - 1]
    total = total / full
    mean, square, grad_mean, cross = (total[i : i + 1, :] for i in range(4))
    rstd = lax.rsqrt(square - mean * mean + EPS)
    shift = -mean * rstd
    proj = rstd * (cross - mean * grad_mean)

    for h in range(heads):
        attended = o_ref[h]
        normed = attended * rstd + shift
        out_ref[:, cols(h)] = (normed.T * gain_ref[:, cols(h)]).astype(BF16)
        grad = rstd * (sc_ref[h] - grad_mean - normed * proj)
        sc_ref[h] = grad
        grad = (grad * far_scale[h]).astype(BF16)
        delta = jnp.sum(grad.astype(F32) * attended, axis=0, keepdims=True)
        far_k = far_ref[:, :, cols(h)].reshape(far_rows, HEAD_FEATURES)
        far_v = far_ref[:, :, wide_cols(h)].reshape(far_rows, HEAD_FEATURES)
        weight = pf_ref[h]
        slope = (weight.astype(F32) * (dot(far_v, grad) - delta)).astype(BF16)
        dqf_ref[h] = dot(far_k, slope, 0, 0)
        key_term = dot(slope, q_ref[:, cols(h)]) * scale
        value_term = dot(weight, grad, 1, 1)
        own_ref[:, cols(h)] = key_term[0:picked]
        own_ref[:, wide_cols(h)] = value_term[0:picked]
        part, spot = divmod(h, part_heads)
        term_ref[part, :, :, cols(spot)] = (
            key_term[picked:].astype(BF16).reshape(reach, picked, HEAD_FEATURES)
        )
        term_ref[part, :, :, cols(spot + part_heads)] = (
            value_term[picked:].astype(BF16).reshape(reach, picked, HEAD_FEATURES)
        )
        if spot == part_heads - 1:
            for d in reversed(range(1, slots)):
                @pl.when(c >= d)
                def _():
                    back_copy(part, d).start()

    for h in range(early):
        for low, high, key_part, value_part in near_backward(
            h, q_ref, k_ref, v_ref, p_ref, ds_ref, sc_ref, o_ref, dqf_ref, near_ref, dq_ref
        ):
            dkn_ref[low:high, cols(h)] = key_part
            dvn_ref[low:high, cols(h)] = value_part

    for part in range(halves):
        for d in range(1, slots):
            @pl.when(c + d < ctx_size)
            def _():
                back_copy(part, d).wait_recv()
        theirs = back_ref[part, 0].astype(F32)
        for d in range(2, slots):
            theirs = theirs + back_ref[part, d - 1].astype(F32)
        for inner in range(part_heads):
            h = part * part_heads + inner
            own_ref[:, cols(h)] = own_ref[:, cols(h)] + theirs[:, cols(inner)]
            own_ref[:, wide_cols(h)] = (
                own_ref[:, wide_cols(h)] + theirs[:, cols(inner + part_heads)]
            )

    for d in range(1, slots):
        @pl.when(c + d < ctx_size)
        def _():
            far_copy(d).wait_send()

        @pl.when(c >= d)
        def _():
            for part in range(halves):
                back_copy(part, d).wait_send()
    for e in range(1, head_size):
        stat_copy(e).wait_send()


def finish(
    out_ref, dqe_ref, dkn_ref, dvn_ref, own_ref,
    q_ref, k_ref, v_ref, p_ref, sc_ref, o_ref, dqf_ref, near_ref,
    out_hbm, dq_hbm, dk_hbm, dv_hbm,
    dq_ref, dk_ref, dv_ref, ds_ref, out_sem, head_sem,
):
    toks, width = q_ref.shape
    heads = width // HEAD_FEATURES
    picked = own_ref.shape[0]
    early = dkn_ref.shape[1] // HEAD_FEATURES
    copies = [pltpu.make_async_copy(out_ref, out_hbm, out_sem.at[0])]
    copies[0].start()

    def send(h, i, source, target):
        copy = pltpu.make_async_copy(
            source.at[:, cols(h)], target.at[:, cols(h)], head_sem.at[h, i]
        )
        copy.start()
        copies.append(copy)

    for h in range(early):
        send(h, 0, dqe_ref, dq_hbm)
    spot = iota((toks, 2 * picked), 0)
    target = iota((toks, 2 * picked), 1) % picked * DILATION
    for h in range(heads):
        offset = lax.rem(lax.axis_index("head") * heads + h, DILATION)
        place = jnp.where(spot == target + offset, 1.0, 0.0).astype(BF16)
        wholes = []
        for column in (h, heads + h):
            mine = own_ref[:, cols(column)]
            upper = mine.astype(BF16)
            lower = (mine - upper.astype(F32)).astype(BF16)
            wholes.append(jnp.concatenate([upper, lower], axis=0))
        if h < early:
            parts = [
                (low, high, dkn_ref[low:high, cols(h)], dvn_ref[low:high, cols(h)])
                for low, high in blocks_of(toks)
            ]
        else:
            parts = near_backward(
                h, q_ref, k_ref, v_ref, p_ref, ds_ref, sc_ref, o_ref, dqf_ref, near_ref, dq_ref
            )
            send(h, 0, dq_ref, dq_hbm)
        for low, high, key_part, value_part in parts:
            rows = place[low:high]
            dk_ref[low:high, cols(h)] = (key_part + dot(rows, wholes[0])).astype(BF16)
            dv_ref[low:high, cols(h)] = (value_part + dot(rows, wholes[1])).astype(BF16)
        send(h, 1, dk_ref, dk_hbm)
        send(h, 2, dv_ref, dv_hbm)
    for copy in copies:
        copy.wait()


def shards(queries, keys, values, out_grad, norm_gain, doc_lengths, group_level):
    toks, width = queries.shape
    heads = width // HEAD_FEATURES
    ctx_size, head_size = lax.axis_size("ctx"), lax.axis_size("head")
    group_heads = heads * head_size // group_level.shape[0]
    picked = toks // DILATION
    reach = max(ctx_size // 2, 1)
    slots = reach + 1
    early = heads // 2
    vmem = pl.BlockSpec(memory_space=pltpu.VMEM)
    hbm = pl.BlockSpec(memory_space=pltpu.HBM)
    halves = 2 if heads % 2 == 0 else 1
    grads = jax.ShapeDtypeStruct((toks, width), BF16)
    across = (heads, HEAD_FEATURES, toks)
    held = (
        pltpu.VMEM((toks, width), BF16),
        pltpu.VMEM((toks, width), BF16),
        pltpu.VMEM((toks, early * HEAD_FEATURES), F32),
        pltpu.VMEM((toks, early * HEAD_FEATURES), F32),
        pltpu.VMEM((picked, 2 * width), F32),
        pltpu.VMEM((toks, width), BF16),
        pltpu.VMEM((toks, width), BF16),
        pltpu.VMEM((toks, width), BF16),
        pltpu.VMEM((heads, toks, toks), BF16),
        pltpu.VMEM(across, F32),
        pltpu.VMEM(across, F32),
        pltpu.VMEM(across, F32),
        pltpu.VMEM((heads, 1, toks), F32),
    )
    gain = norm_gain.reshape(1, width)
    operands = (queries, keys, values, out_grad, gain, doc_lengths, group_level)
    results = pl.pallas_call(
        functools.partial(kernel, ctx_size, head_size, reach, group_heads),
        out_shape=held,
        in_specs=[hbm] * 7,
        out_specs=(vmem,) * len(held),
        scratch_shapes=[
            pltpu.VMEM((slots, picked, 2 * width), BF16),
            pltpu.VMEM((halves, reach, picked, 2 * width // halves), BF16),
            pltpu.VMEM((halves, reach, picked, 2 * width // halves), BF16),
            pltpu.VMEM((8, toks), F32),
            pltpu.VMEM((head_size - 1, 8, toks), F32),
            pltpu.VMEM((toks, width), BF16),
            pltpu.VMEM((1, width), F32),
            pltpu.SMEM(doc_lengths.shape, jnp.int32),
            pltpu.SMEM(group_level.shape, jnp.int32),
            pltpu.SemaphoreType.DMA((7,)),
            pltpu.VMEM((toks, toks), F32),
            pltpu.VMEM((heads, slots * picked, toks), BF16),
            pltpu.VMEM((toks, toks), BF16),
            pltpu.SemaphoreType.DMA((reach,)),
            pltpu.SemaphoreType.DMA((reach,)),
            pltpu.SemaphoreType.DMA((halves, reach)),
            pltpu.SemaphoreType.DMA((halves, reach)),
            pltpu.SemaphoreType.DMA((head_size - 1,)),
            pltpu.SemaphoreType.DMA((head_size - 1,)),
        ],
        compiler_params=pltpu.CompilerParams(
            collective_id=0, has_side_effects=True, vmem_limit_bytes=32 * 1024 * 1024
        ),
    )(*(pltpu.with_memory_space_constraint(given, pltpu.HBM) for given in operands))
    return pl.pallas_call(
        finish,
        out_shape=(grads,) * 4,
        in_specs=[vmem] * len(held),
        out_specs=(hbm,) * 4,
        scratch_shapes=[
            pltpu.VMEM((toks, width), BF16),
            pltpu.VMEM((toks, width), BF16),
            pltpu.VMEM((toks, width), BF16),
            pltpu.VMEM((toks, toks), BF16),
            pltpu.SemaphoreType.DMA((1,)),
            pltpu.SemaphoreType.DMA((heads, 3)),
        ],
        compiler_params=pltpu.CompilerParams(vmem_limit_bytes=24 * 1024 * 1024),
    )(*results)


def solution(mesh):
    split = P("ctx", "head")
    return jax.shard_map(
        shards,
        mesh=mesh,
        in_specs=(split, split, split, split, P("head"), P(), P()),
        out_specs=(split, split, split, split),
        check_vma=False,
    )
```

```python
import functools
import math

import jax
import jax.numpy as jnp
from jax import lax
from jax.experimental import pallas as pl
from jax.experimental.pallas import tpu as pltpu
from jax.sharding import PartitionSpec as P

HEAD_FEATURES = 128
DILATION = 32
EPS = 1e-05
HIDDEN = -1e30
MESH = pl.DeviceIdType.MESH
F32 = jnp.float32
BF16 = jnp.bfloat16


def dot(a, b, left=1, right=0):
    return lax.dot_general(a, b, (((left,), (right,)), ((), ())), preferred_element_type=F32)


def iota(shape, dim):
    return lax.broadcasted_iota(jnp.int32, shape, dim)


def cols(h):
    return slice(h * HEAD_FEATURES, (h + 1) * HEAD_FEATURES)


def blocks_of(toks):
    return [(0, toks // 2), (toks // 2, toks)]


def near_backward(h, q_ref, k_ref, v_ref, p_ref, ds_ref, sc_ref, o_ref, dqf_ref, near_ref, dq_ref):
    toks = q_ref.shape[0]
    blocks = blocks_of(toks)
    scale = HEAD_FEATURES ** (-0.5)
    grad = (sc_ref[h] * near_ref[h]).astype(BF16)
    delta = jnp.sum(grad.astype(F32) * o_ref[h], axis=0, keepdims=True)
    keys_t = k_ref[:, cols(h)].T
    for low, high in blocks:
        product = dot(v_ref[0:high, cols(h)], grad[:, low:high])
        weight = p_ref[h, 0:high, low:high].astype(F32)
        slope = (weight * (product - delta[:, low:high])).astype(BF16)
        ds_ref[0:high, low:high] = slope
        query_grad = dot(keys_t[:, 0:high], slope) + dqf_ref[h, :, low:high]
        dq_ref[low:high, cols(h)] = (query_grad * scale).T.astype(BF16)
    return [
        (
            low,
            high,
            dot(ds_ref[low:high, low:toks], q_ref[low:toks, cols(h)]) * scale,
            dot(p_ref[h, low:high, low:toks], grad[:, low:toks], 1, 1),
        )
        for low, high in blocks
    ]


def kernel(
    ctx_size, head_size, reach, group_heads,
    q_hbm, k_hbm, v_hbm, og_hbm, gain_hbm, len_hbm, level_hbm,
    out_ref, dq_ref, dkn_ref, dvn_ref, own_ref,
    q_ref, k_ref, v_ref, p_ref, sc_ref, o_ref, dqf_ref, near_ref,
    far_ref, term_ref, back_ref, stat_ref, stats_ref,
    og_ref, gain_ref, len_ref, level_ref, load_sem,
    bias_ref, pf_ref, ds_ref,
    far_send, far_recv, back_send, back_recv, stat_send, stat_recv,
):
    loads = [
        pltpu.make_async_copy(source, target, load_sem.at[i])
        for i, (source, target) in enumerate(
            (
                (k_hbm, k_ref), (v_hbm, v_ref), (len_hbm, len_ref), (level_hbm, level_ref),
                (q_hbm, q_ref), (gain_hbm, gain_ref), (og_hbm, og_ref),
            )
        )
    ]
    for load in loads[:4]:
        load.start()
    toks, width = q_ref.shape
    heads = width // HEAD_FEATURES
    picked = toks // DILATION
    slots = reach + 1
    far_rows = slots * picked
    half = toks // 2
    early = dkn_ref.shape[1] // HEAD_FEATURES
    full = width * head_size
    scale = HEAD_FEATURES ** (-0.5)
    scale2 = scale * math.log2(math.e)
    c = lax.axis_index("ctx")
    hp = lax.axis_index("head")

    def wide_cols(h):
        return slice(width + h * HEAD_FEATURES, width + (h + 1) * HEAD_FEATURES)

    parts_back = back_ref.shape[0]
    part_heads = heads // parts_back
    far_parts = far_ref.shape[0]
    far_heads = heads // far_parts

    blocks = blocks_of(toks)

    barrier = pltpu.get_barrier_semaphore()
    for d in range(1, slots):
        @pl.when(c + d < ctx_size)
        def _():
            pl.semaphore_signal(barrier, inc=1, device_id=(c + d, hp), device_id_type=MESH)

        @pl.when(c >= d)
        def _():
            pl.semaphore_signal(barrier, inc=1, device_id=(c - d, hp), device_id_type=MESH)
    for e in range(1, head_size):
        peer = lax.rem(hp + e, head_size)
        pl.semaphore_signal(barrier, inc=1, device_id=(c, peer), device_id_type=MESH)

    for d in range(1, slots):
        @pl.when(c < d)
        def _():
            far_ref[:, d] = jnp.zeros((far_parts,) + far_ref.shape[2:], BF16)

        @pl.when(c + d >= ctx_size)
        def _():
            back_ref[:, d - 1] = jnp.zeros((parts_back,) + back_ref.shape[2:], BF16)

    loads[0].wait()
    loads[1].wait()
    for load in loads[4:]:
        load.start()

    def offset_of(h):
        return lax.rem(hp * heads + h, DILATION)

    row_of = iota((picked, toks), 0) * DILATION
    place_in = iota((picked, toks), 1)
    def pick_part(part):
        for spot in range(far_heads):
            h = part * far_heads + spot
            pick = jnp.where(place_in == row_of + offset_of(h), 1.0, 0.0).astype(BF16)
            far_ref[part, 0, :, cols(spot)] = dot(pick, k_ref[:, cols(h)]).astype(BF16)
            far_ref[part, 0, :, cols(spot + far_heads)] = dot(pick, v_ref[:, cols(h)]).astype(BF16)

    def far_rows_of(h):
        part, spot = divmod(h, far_heads)
        shape = (far_rows, HEAD_FEATURES)
        return (
            far_ref[part, :, :, cols(spot)].reshape(shape),
            far_ref[part, :, :, cols(spot + far_heads)].reshape(shape),
        )

    def far_copy(part, d):
        return pltpu.make_async_remote_copy(
            src_ref=far_ref.at[part, 0], dst_ref=far_ref.at[part, d],
            send_sem=far_send.at[part, d - 1], recv_sem=far_recv.at[part, d - 1],
            device_id=(c + d, hp), device_id_type=MESH,
        )

    before = jnp.minimum(c, reach)
    after = jnp.minimum(ctx_size - 1 - c, reach)
    for part in range(far_parts):
        pick_part(part)
        if part == 0:
            pl.semaphore_wait(barrier, before + after + (head_size - 1))
        for d in range(1, slots):
            @pl.when(c + d < ctx_size)
            def _():
                far_copy(part, d).start()

    def back_copy(part, d):
        return pltpu.make_async_remote_copy(
            src_ref=term_ref.at[part, d - 1], dst_ref=back_ref.at[part, d - 1],
            send_sem=back_send.at[part, d - 1], recv_sem=back_recv.at[part, d - 1],
            device_id=(c - d, hp), device_id_type=MESH,
        )

    def stat_copy(e):
        return pltpu.make_async_remote_copy(
            src_ref=stat_ref, dst_ref=stats_ref.at[e - 1],
            send_sem=stat_send.at[e - 1], recv_sem=stat_recv.at[e - 1],
            device_id=(c, lax.rem(hp + e, head_size)), device_id_type=MESH,
        )

    for load in loads[2:]:
        load.wait()

    place_q = iota((1, toks), 1) + c * toks
    first = jnp.zeros((1, toks), jnp.int32)
    end = jnp.int32(0)
    for i in range(len_ref.shape[0]):
        end = end + len_ref[i]
        first = jnp.maximum(first, jnp.where(place_q >= end, end, 0))
    for low, high in blocks:
        place_k = iota((high, half), 0) + c * toks
        seen = (place_k <= place_q[:, low:high]) & (place_k >= first[:, low:high])
        bias_ref[0:high, low:high] = jnp.where(seen, 0.0, HIDDEN)

    tops, sums = [], []
    scaled_sum = jnp.zeros((1, toks), F32)
    for h in range(heads):
        values_t = v_ref[:, cols(h)].T
        top_parts, sum_parts = [], []
        for low, high in blocks:
            logit = dot(k_ref[0:high, cols(h)], q_ref[low:high, cols(h)], 1, 1)
            logit = logit * scale2 + bias_ref[0:high, low:high]
            top = jnp.max(logit, axis=0, keepdims=True)
            weight = jnp.exp2(logit - top)
            top_parts.append(top)
            sum_parts.append(jnp.sum(weight, axis=0, keepdims=True))
            weight = weight.astype(BF16)
            p_ref[h, 0:high, low:high] = weight
            o_ref[h, :, low:high] = dot(values_t[:, 0:high], weight)
        tops.append(jnp.concatenate(top_parts, axis=1))
        sums.append(jnp.concatenate(sum_parts, axis=1))
        scaled = og_ref[:, cols(h)].astype(F32) * gain_ref[:, cols(h)]
        scaled = scaled.T
        sc_ref[h] = scaled
        scaled_sum = scaled_sum + jnp.sum(scaled, axis=0, keepdims=True)

    row = iota((far_rows, toks), 0)
    counter = (c - row // picked) * picked + row % picked
    near_scale, far_scale = [], []
    stats = [jnp.zeros((1, toks), F32) for _ in range(3)]
    for h in range(heads):
        if h % far_heads == 0:
            for d in range(1, slots):
                @pl.when(c >= d)
                def _():
                    far_copy(h // far_heads, d).wait_recv()
        far_k, far_v = far_rows_of(h)
        level = level_ref[(hp * heads + h) // group_heads]
        skip = jnp.left_shift(jnp.int32(1), level) - 1
        place_k = counter * DILATION + offset_of(h)
        seen = (place_k <= place_q) & (place_k >= first) & ((counter & skip) == 0)
        logit = jnp.where(seen, dot(far_k, q_ref[:, cols(h)], 1, 1) * scale2, HIDDEN)
        top = jnp.maximum(tops[h], jnp.max(logit, axis=0, keepdims=True))
        weight = jnp.exp2(logit - top)
        shrink = jnp.exp2(tops[h] - top)
        inverse = 1.0 / (sums[h] * shrink + jnp.sum(weight, axis=0, keepdims=True))
        weight = weight.astype(BF16)
        pf_ref[h] = weight
        near_scale.append(shrink * inverse)
        near_ref[h] = near_scale[h]
        far_scale.append(inverse)
        attended = (o_ref[h] * near_scale[h] + dot(far_v, weight, 0, 0) * inverse).astype(BF16)
        attended = attended.astype(F32)
        o_ref[h] = attended
        scaled = sc_ref[h]
        terms = (attended, attended * attended, scaled * attended)
        stats = [s + jnp.sum(t, axis=0, keepdims=True) for s, t in zip(stats, terms)]

    stats.append(scaled_sum)
    for i in range(4):
        stat_ref[i : i + 1, :] = stats[i]
    stat_ref[4:8, :] = jnp.zeros((4, toks), F32)
    for e in range(1, head_size):
        stat_copy(e).start()
    for e in range(1, head_size):
        stat_copy(e).wait_recv()
    total = stat_ref[...]
    for e in range(1, head_size):
        total = total + stats_ref[e - 1]
    total = total / full
    mean, square, cross, grad_mean = (total[i : i + 1, :] for i in range(4))
    rstd = lax.rsqrt(square - mean * mean + EPS)
    shift = -mean * rstd
    proj = rstd * (cross - mean * grad_mean)

    for h in range(heads):
        attended = o_ref[h]
        normed = attended * rstd + shift
        grad = rstd * (sc_ref[h] - grad_mean - normed * proj)
        sc_ref[h] = grad
        grad = (grad * far_scale[h]).astype(BF16)
        delta = jnp.sum(grad.astype(F32) * attended, axis=0, keepdims=True)
        far_v = far_rows_of(h)[1]
        weight = pf_ref[h]
        slope = (weight.astype(F32) * (dot(far_v, grad) - delta)).astype(BF16)
        key_term = dot(slope, q_ref[:, cols(h)]) * scale
        value_term = dot(weight, grad, 1, 1)
        pf_ref[h] = slope
        own_ref[:, cols(h)] = key_term[0:picked]
        own_ref[:, wide_cols(h)] = value_term[0:picked]
        part, spot = divmod(h, part_heads)
        term_ref[part, :, :, cols(spot)] = (
            key_term[picked:].astype(BF16).reshape(reach, picked, HEAD_FEATURES)
        )
        term_ref[part, :, :, cols(spot + part_heads)] = (
            value_term[picked:].astype(BF16).reshape(reach, picked, HEAD_FEATURES)
        )
        if spot == part_heads - 1:
            for d in reversed(range(1, slots)):
                @pl.when(c >= d)
                def _():
                    back_copy(part, d).start()

    for h in range(heads):
        dqf_ref[h] = dot(far_rows_of(h)[0], pf_ref[h], 0, 0)
        normed = o_ref[h] * rstd + shift
        out_ref[:, cols(h)] = (normed.T * gain_ref[:, cols(h)]).astype(BF16)

    for h in range(early):
        for low, high, key_part, value_part in near_backward(
            h, q_ref, k_ref, v_ref, p_ref, ds_ref, sc_ref, o_ref, dqf_ref, near_ref, dq_ref
        ):
            dkn_ref[low:high, cols(h)] = key_part
            dvn_ref[low:high, cols(h)] = value_part

    for part in range(parts_back):
        for d in range(1, slots):
            @pl.when(c + d < ctx_size)
            def _():
                back_copy(part, d).wait_recv()
        theirs = back_ref[part, 0].astype(F32)
        for d in range(2, slots):
            theirs = theirs + back_ref[part, d - 1].astype(F32)
        for inner in range(part_heads):
            h = part * part_heads + inner
            own_ref[:, cols(h)] = own_ref[:, cols(h)] + theirs[:, cols(inner)]
            own_ref[:, wide_cols(h)] = (
                own_ref[:, wide_cols(h)] + theirs[:, cols(inner + part_heads)]
            )

    for d in range(1, slots):
        @pl.when(c + d < ctx_size)
        def _():
            for part in range(far_parts):
                far_copy(part, d).wait_send()

        @pl.when(c >= d)
        def _():
            for part in range(parts_back):
                back_copy(part, d).wait_send()
    for e in range(1, head_size):
        stat_copy(e).wait_send()


def finish(
    out_ref, dqe_ref, dkn_ref, dvn_ref, own_ref,
    q_ref, k_ref, v_ref, p_ref, sc_ref, o_ref, dqf_ref, near_ref,
    out_hbm, dq_hbm, dk_hbm, dv_hbm,
    dq_ref, dk_ref, dv_ref, ds_ref, out_sem, head_sem,
):
    toks, width = q_ref.shape
    heads = width // HEAD_FEATURES
    picked = own_ref.shape[0]
    early = dkn_ref.shape[1] // HEAD_FEATURES
    copies = [pltpu.make_async_copy(out_ref, out_hbm, out_sem.at[0])]
    copies[0].start()

    def send(h, i, source, target):
        copy = pltpu.make_async_copy(
            source.at[:, cols(h)], target.at[:, cols(h)], head_sem.at[h, i]
        )
        copy.start()
        copies.append(copy)

    for h in range(early):
        send(h, 0, dqe_ref, dq_hbm)
    spot = iota((toks, 2 * picked), 0)
    target = iota((toks, 2 * picked), 1) % picked * DILATION
    for h in range(heads):
        offset = lax.rem(lax.axis_index("head") * heads + h, DILATION)
        place = jnp.where(spot == target + offset, 1.0, 0.0).astype(BF16)
        wholes = []
        for column in (h, heads + h):
            mine = own_ref[:, cols(column)]
            upper = mine.astype(BF16)
            lower = (mine - upper.astype(F32)).astype(BF16)
            wholes.append(jnp.concatenate([upper, lower], axis=0))
        if h < early:
            parts = [
                (low, high, dkn_ref[low:high, cols(h)], dvn_ref[low:high, cols(h)])
                for low, high in blocks_of(toks)
            ]
        else:
            parts = near_backward(
                h, q_ref, k_ref, v_ref, p_ref, ds_ref, sc_ref, o_ref, dqf_ref, near_ref, dq_ref
            )
            send(h, 0, dq_ref, dq_hbm)
        for low, high, key_part, value_part in parts:
            rows = place[low:high]
            dk_ref[low:high, cols(h)] = (key_part + dot(rows, wholes[0])).astype(BF16)
            dv_ref[low:high, cols(h)] = (value_part + dot(rows, wholes[1])).astype(BF16)
        send(h, 1, dk_ref, dk_hbm)
        send(h, 2, dv_ref, dv_hbm)
    for copy in copies:
        copy.wait()


def shards(queries, keys, values, out_grad, norm_gain, doc_lengths, group_level):
    toks, width = queries.shape
    heads = width // HEAD_FEATURES
    ctx_size, head_size = lax.axis_size("ctx"), lax.axis_size("head")
    group_heads = heads * head_size // group_level.shape[0]
    picked = toks // DILATION
    reach = max(ctx_size // 2, 1)
    slots = reach + 1
    early = heads - heads // 4
    vmem = pl.BlockSpec(memory_space=pltpu.VMEM)
    hbm = pl.BlockSpec(memory_space=pltpu.HBM)
    far_parts = 2 if heads % 2 == 0 else 1
    parts_back = heads
    grads = jax.ShapeDtypeStruct((toks, width), BF16)
    across = (heads, HEAD_FEATURES, toks)
    held = (
        pltpu.VMEM((toks, width), BF16),
        pltpu.VMEM((toks, width), BF16),
        pltpu.VMEM((toks, early * HEAD_FEATURES), F32),
        pltpu.VMEM((toks, early * HEAD_FEATURES), F32),
        pltpu.VMEM((picked, 2 * width), F32),
        pltpu.VMEM((toks, width), BF16),
        pltpu.VMEM((toks, width), BF16),
        pltpu.VMEM((toks, width), BF16),
        pltpu.VMEM((heads, toks, toks), BF16),
        pltpu.VMEM(across, F32),
        pltpu.VMEM(across, F32),
        pltpu.VMEM(across, F32),
        pltpu.VMEM((heads, 1, toks), F32),
    )
    gain = norm_gain.reshape(1, width)
    operands = (queries, keys, values, out_grad, gain, doc_lengths, group_level)
    results = pl.pallas_call(
        functools.partial(kernel, ctx_size, head_size, reach, group_heads),
        out_shape=held,
        in_specs=[hbm] * 7,
        out_specs=(vmem,) * len(held),
        scratch_shapes=[
            pltpu.VMEM((far_parts, slots, picked, 2 * width // far_parts), BF16),
            pltpu.VMEM((parts_back, reach, picked, 2 * width // parts_back), BF16),
            pltpu.VMEM((parts_back, reach, picked, 2 * width // parts_back), BF16),
            pltpu.VMEM((8, toks), F32),
            pltpu.VMEM((head_size - 1, 8, toks), F32),
            pltpu.VMEM((toks, width), BF16),
            pltpu.VMEM((1, width), F32),
            pltpu.SMEM(doc_lengths.shape, jnp.int32),
            pltpu.SMEM(group_level.shape, jnp.int32),
            pltpu.SemaphoreType.DMA((7,)),
            pltpu.VMEM((toks, toks), F32),
            pltpu.VMEM((heads, slots * picked, toks), BF16),
            pltpu.VMEM((toks, toks), BF16),
            pltpu.SemaphoreType.DMA((far_parts, reach)),
            pltpu.SemaphoreType.DMA((far_parts, reach)),
            pltpu.SemaphoreType.DMA((parts_back, reach)),
            pltpu.SemaphoreType.DMA((parts_back, reach)),
            pltpu.SemaphoreType.DMA((head_size - 1,)),
            pltpu.SemaphoreType.DMA((head_size - 1,)),
        ],
        compiler_params=pltpu.CompilerParams(
            collective_id=0, has_side_effects=True, vmem_limit_bytes=32 * 1024 * 1024
        ),
    )(*(pltpu.with_memory_space_constraint(given, pltpu.HBM) for given in operands))
    return pl.pallas_call(
        finish,
        out_shape=(grads,) * 4,
        in_specs=[vmem] * len(held),
        out_specs=(hbm,) * 4,
        scratch_shapes=[
            pltpu.VMEM((toks, width), BF16),
            pltpu.VMEM((toks, width), BF16),
            pltpu.VMEM((toks, width), BF16),
            pltpu.VMEM((toks, toks), BF16),
            pltpu.SemaphoreType.DMA((1,)),
            pltpu.SemaphoreType.DMA((heads, 3)),
        ],
        compiler_params=pltpu.CompilerParams(vmem_limit_bytes=24 * 1024 * 1024),
    )(*results)


def solution(mesh):
    split = P("ctx", "head")
    return jax.shard_map(
        shards,
        mesh=mesh,
        in_specs=(split, split, split, split, P("head"), P(), P()),
        out_specs=(split, split, split, split),
        check_vma=False,
    )
```

```python
import functools
import math

import jax
import jax.numpy as jnp
from jax import lax
from jax.experimental import pallas as pl
from jax.experimental.pallas import tpu as pltpu
from jax.sharding import PartitionSpec as P

HEAD_FEATURES = 128
DILATION = 32
EPS = 1e-05
HIDDEN = -1e30
MESH = pl.DeviceIdType.MESH
F32 = jnp.float32
BF16 = jnp.bfloat16


def dot(a, b, left=1, right=0):
    return lax.dot_general(a, b, (((left,), (right,)), ((), ())), preferred_element_type=F32)


def iota(shape, dim):
    return lax.broadcasted_iota(jnp.int32, shape, dim)


def cols(h):
    return slice(h * HEAD_FEATURES, (h + 1) * HEAD_FEATURES)


def blocks_of(toks):
    return [(0, toks // 2), (toks // 2, toks)]


def near_backward(h, q_ref, k_ref, v_ref, p_ref, ds_ref, sc_ref, o_ref, dqf_ref, near_ref, dq_ref):
    toks = q_ref.shape[0]
    blocks = blocks_of(toks)
    scale = HEAD_FEATURES ** (-0.5)
    grad = (sc_ref[h] * near_ref[h]).astype(BF16)
    delta = jnp.sum(grad.astype(F32) * o_ref[h], axis=0, keepdims=True)
    keys_t = k_ref[:, cols(h)].T
    for low, high in blocks:
        product = dot(v_ref[0:high, cols(h)], grad[:, low:high])
        weight = p_ref[h, 0:high, low:high].astype(F32)
        slope = (weight * (product - delta[:, low:high])).astype(BF16)
        ds_ref[0:high, low:high] = slope
        query_grad = dot(keys_t[:, 0:high], slope) + dqf_ref[h, :, low:high]
        dq_ref[low:high, cols(h)] = (query_grad * scale).T.astype(BF16)
    return [
        (
            low,
            high,
            dot(ds_ref[low:high, low:toks], q_ref[low:toks, cols(h)]) * scale,
            dot(p_ref[h, low:high, low:toks], grad[:, low:toks], 1, 1),
        )
        for low, high in blocks
    ]


def kernel(
    ctx_size, head_size, reach, group_heads,
    q_hbm, k_hbm, v_hbm, og_hbm, gain_hbm, len_hbm, level_hbm,
    out_ref, dq_ref, dkn_ref, dvn_ref, own_ref,
    q_ref, k_ref, v_ref, p_ref, sc_ref, o_ref, dqf_ref, near_ref,
    far_ref, term_ref, back_ref, stat_ref, stats_ref,
    og_ref, gain_ref, len_ref, level_ref, load_sem,
    bias_ref, pf_ref, ds_ref,
    far_send, far_recv, back_send, back_recv, stat_send, stat_recv,
):
    loads = [
        pltpu.make_async_copy(source, target, load_sem.at[i])
        for i, (source, target) in enumerate(
            (
                (k_hbm, k_ref), (v_hbm, v_ref), (len_hbm, len_ref), (level_hbm, level_ref),
                (q_hbm, q_ref), (gain_hbm, gain_ref), (og_hbm, og_ref),
            )
        )
    ]
    for load in loads[:4]:
        load.start()
    toks, width = q_ref.shape
    heads = width // HEAD_FEATURES
    picked = toks // DILATION
    slots = reach + 1
    far_rows = slots * picked
    half = toks // 2
    early = dkn_ref.shape[1] // HEAD_FEATURES
    full = width * head_size
    scale = HEAD_FEATURES ** (-0.5)
    scale2 = scale * math.log2(math.e)
    c = lax.axis_index("ctx")
    hp = lax.axis_index("head")

    def wide_cols(h):
        return slice(width + h * HEAD_FEATURES, width + (h + 1) * HEAD_FEATURES)

    parts_back = back_ref.shape[0]
    part_heads = heads // parts_back
    far_parts = far_ref.shape[0]
    far_heads = heads // far_parts

    blocks = blocks_of(toks)

    barrier = pltpu.get_barrier_semaphore()
    for d in range(1, slots):
        @pl.when(c + d < ctx_size)
        def _():
            pl.semaphore_signal(barrier, inc=1, device_id=(c + d, hp), device_id_type=MESH)

        @pl.when(c >= d)
        def _():
            pl.semaphore_signal(barrier, inc=1, device_id=(c - d, hp), device_id_type=MESH)
    for e in range(1, head_size):
        peer = lax.rem(hp + e, head_size)
        pl.semaphore_signal(barrier, inc=1, device_id=(c, peer), device_id_type=MESH)

    for d in range(1, slots):
        @pl.when(c < d)
        def _():
            far_ref[:, d] = jnp.zeros((far_parts,) + far_ref.shape[2:], BF16)

        @pl.when(c + d >= ctx_size)
        def _():
            back_ref[:, d - 1] = jnp.zeros((parts_back,) + back_ref.shape[2:], BF16)

    loads[0].wait()
    loads[1].wait()
    for load in loads[4:]:
        load.start()

    def offset_of(h):
        return lax.rem(hp * heads + h, DILATION)

    row_of = iota((picked, toks), 0) * DILATION
    place_in = iota((picked, toks), 1)
    def pick_part(part):
        for spot in range(far_heads):
            h = part * far_heads + spot
            pick = jnp.where(place_in == row_of + offset_of(h), 1.0, 0.0).astype(BF16)
            far_ref[part, 0, :, cols(spot)] = dot(pick, k_ref[:, cols(h)]).astype(BF16)
            far_ref[part, 0, :, cols(spot + far_heads)] = dot(pick, v_ref[:, cols(h)]).astype(BF16)

    def far_rows_of(h):
        part, spot = divmod(h, far_heads)
        shape = (far_rows, HEAD_FEATURES)
        return (
            far_ref[part, :, :, cols(spot)].reshape(shape),
            far_ref[part, :, :, cols(spot + far_heads)].reshape(shape),
        )

    def far_copy(part, d):
        return pltpu.make_async_remote_copy(
            src_ref=far_ref.at[part, 0], dst_ref=far_ref.at[part, d],
            send_sem=far_send.at[part, d - 1], recv_sem=far_recv.at[part, d - 1],
            device_id=(c + d, hp), device_id_type=MESH,
        )

    before = jnp.minimum(c, reach)
    after = jnp.minimum(ctx_size - 1 - c, reach)
    for part in range(far_parts):
        pick_part(part)
        if part == 0:
            pl.semaphore_wait(barrier, before + after + (head_size - 1))
        for d in range(1, slots):
            @pl.when(c + d < ctx_size)
            def _():
                far_copy(part, d).start()

    def back_copy(part, d):
        return pltpu.make_async_remote_copy(
            src_ref=term_ref.at[part, d - 1], dst_ref=back_ref.at[part, d - 1],
            send_sem=back_send.at[part, d - 1], recv_sem=back_recv.at[part, d - 1],
            device_id=(c - d, hp), device_id_type=MESH,
        )

    def stat_copy(e):
        return pltpu.make_async_remote_copy(
            src_ref=stat_ref, dst_ref=stats_ref.at[e - 1],
            send_sem=stat_send.at[e - 1], recv_sem=stat_recv.at[e - 1],
            device_id=(c, lax.rem(hp + e, head_size)), device_id_type=MESH,
        )

    for load in loads[2:]:
        load.wait()

    place_q = iota((1, toks), 1) + c * toks
    first = jnp.zeros((1, toks), jnp.int32)
    end = jnp.int32(0)
    for i in range(len_ref.shape[0]):
        end = end + len_ref[i]
        first = jnp.maximum(first, jnp.where(place_q >= end, end, 0))
    for low, high in blocks:
        place_k = iota((high, half), 0) + c * toks
        seen = (place_k <= place_q[:, low:high]) & (place_k >= first[:, low:high])
        bias_ref[0:high, low:high] = jnp.where(seen, 0.0, HIDDEN)

    tops, sums = [], []
    scaled_sum = jnp.zeros((1, toks), F32)
    for h in range(heads):
        values_t = v_ref[:, cols(h)].T
        top_parts, sum_parts = [], []
        for low, high in blocks:
            logit = dot(k_ref[0:high, cols(h)], q_ref[low:high, cols(h)], 1, 1)
            logit = logit * scale2 + bias_ref[0:high, low:high]
            top = jnp.max(logit, axis=0, keepdims=True)
            weight = jnp.exp2(logit - top)
            top_parts.append(top)
            sum_parts.append(jnp.sum(weight, axis=0, keepdims=True))
            weight = weight.astype(BF16)
            p_ref[h, 0:high, low:high] = weight
            o_ref[h, :, low:high] = dot(values_t[:, 0:high], weight)
        tops.append(jnp.concatenate(top_parts, axis=1))
        sums.append(jnp.concatenate(sum_parts, axis=1))
        scaled = og_ref[:, cols(h)].astype(F32) * gain_ref[:, cols(h)]
        scaled = scaled.T
        sc_ref[h] = scaled
        scaled_sum = scaled_sum + jnp.sum(scaled, axis=0, keepdims=True)

    row = iota((far_rows, toks), 0)
    counter = (c - row // picked) * picked + row % picked
    near_scale, far_scale = [], []
    stats = [jnp.zeros((1, toks), F32) for _ in range(3)]
    for h in range(heads):
        if h % far_heads == 0:
            for d in range(1, slots):
                @pl.when(c >= d)
                def _():
                    far_copy(h // far_heads, d).wait_recv()
        far_k, far_v = far_rows_of(h)
        level = level_ref[(hp * heads + h) // group_heads]
        skip = jnp.left_shift(jnp.int32(1), level) - 1
        place_k = counter * DILATION + offset_of(h)
        seen = (place_k <= place_q) & (place_k >= first) & ((counter & skip) == 0)
        logit = jnp.where(seen, dot(far_k, q_ref[:, cols(h)], 1, 1) * scale2, HIDDEN)
        top = jnp.maximum(tops[h], jnp.max(logit, axis=0, keepdims=True))
        weight = jnp.exp2(logit - top)
        shrink = jnp.exp2(tops[h] - top)
        inverse = 1.0 / (sums[h] * shrink + jnp.sum(weight, axis=0, keepdims=True))
        weight = weight.astype(BF16)
        pf_ref[h] = weight
        near_scale.append(shrink * inverse)
        near_ref[h] = near_scale[h]
        far_scale.append(inverse)
        attended = (o_ref[h] * near_scale[h] + dot(far_v, weight, 0, 0) * inverse).astype(BF16)
        attended = attended.astype(F32)
        o_ref[h] = attended
        scaled = sc_ref[h]
        terms = (attended, attended * attended, scaled * attended)
        stats = [s + jnp.sum(t, axis=0, keepdims=True) for s, t in zip(stats, terms)]

    stats.append(scaled_sum)
    for i in range(4):
        stat_ref[i : i + 1, :] = stats[i]
    stat_ref[4:8, :] = jnp.zeros((4, toks), F32)
    for e in range(1, head_size):
        stat_copy(e).start()
    for e in range(1, head_size):
        stat_copy(e).wait_recv()
    total = stat_ref[...]
    for e in range(1, head_size):
        total = total + stats_ref[e - 1]
    total = total / full
    mean, square, cross, grad_mean = (total[i : i + 1, :] for i in range(4))
    rstd = lax.rsqrt(square - mean * mean + EPS)
    shift = -mean * rstd
    proj = rstd * (cross - mean * grad_mean)

    for h in range(heads):
        attended = o_ref[h]
        normed = attended * rstd + shift
        grad = rstd * (sc_ref[h] - grad_mean - normed * proj)
        sc_ref[h] = grad
        grad = (grad * far_scale[h]).astype(BF16)
        delta = jnp.sum(grad.astype(F32) * attended, axis=0, keepdims=True)
        far_v = far_rows_of(h)[1]
        weight = pf_ref[h]
        slope = (weight.astype(F32) * (dot(far_v, grad) - delta)).astype(BF16)
        key_term = dot(slope, q_ref[:, cols(h)]) * scale
        value_term = dot(weight, grad, 1, 1)
        pf_ref[h] = slope
        own_ref[:, cols(h)] = key_term[0:picked]
        own_ref[:, wide_cols(h)] = value_term[0:picked]
        part, spot = divmod(h, part_heads)
        term_ref[part, :, :, cols(spot)] = (
            key_term[picked:].astype(BF16).reshape(reach, picked, HEAD_FEATURES)
        )
        term_ref[part, :, :, cols(spot + part_heads)] = (
            value_term[picked:].astype(BF16).reshape(reach, picked, HEAD_FEATURES)
        )
        if spot == part_heads - 1:
            for d in reversed(range(1, slots)):
                @pl.when(c >= d)
                def _():
                    back_copy(part, d).start()

    for h in range(heads):
        dqf_ref[h] = dot(far_rows_of(h)[0], pf_ref[h], 0, 0)
        normed = o_ref[h] * rstd + shift
        out_ref[:, cols(h)] = (normed.T * gain_ref[:, cols(h)]).astype(BF16)

    for h in range(early):
        for low, high, key_part, value_part in near_backward(
            h, q_ref, k_ref, v_ref, p_ref, ds_ref, sc_ref, o_ref, dqf_ref, near_ref, dq_ref
        ):
            dkn_ref[low:high, cols(h)] = key_part
            dvn_ref[low:high, cols(h)] = value_part

    for part in range(parts_back):
        for d in range(1, slots):
            @pl.when(c + d < ctx_size)
            def _():
                back_copy(part, d).wait_recv()
        theirs = back_ref[part, 0].astype(F32)
        for d in range(2, slots):
            theirs = theirs + back_ref[part, d - 1].astype(F32)
        for inner in range(part_heads):
            h = part * part_heads + inner
            own_ref[:, cols(h)] = own_ref[:, cols(h)] + theirs[:, cols(inner)]
            own_ref[:, wide_cols(h)] = (
                own_ref[:, wide_cols(h)] + theirs[:, cols(inner + part_heads)]
            )

    for d in range(1, slots):
        @pl.when(c + d < ctx_size)
        def _():
            for part in range(far_parts):
                far_copy(part, d).wait_send()

        @pl.when(c >= d)
        def _():
            for part in range(parts_back):
                back_copy(part, d).wait_send()
    for e in range(1, head_size):
        stat_copy(e).wait_send()


def finish(
    out_ref, dqe_ref, dkn_ref, dvn_ref, own_ref,
    q_ref, k_ref, v_ref, p_ref, sc_ref, o_ref, dqf_ref, near_ref,
    out_hbm, dq_hbm, dk_hbm, dv_hbm,
    dq_ref, dk_ref, dv_ref, ds_ref, out_sem, head_sem,
):
    toks, width = q_ref.shape
    heads = width // HEAD_FEATURES
    picked = own_ref.shape[0]
    early = dkn_ref.shape[1] // HEAD_FEATURES
    copies = [pltpu.make_async_copy(out_ref, out_hbm, out_sem.at[0])]
    copies[0].start()

    def send(h, i, source, target):
        copy = pltpu.make_async_copy(
            source.at[:, cols(h)], target.at[:, cols(h)], head_sem.at[h, i]
        )
        copy.start()
        copies.append(copy)

    for h in range(early):
        send(h, 0, dqe_ref, dq_hbm)
    spot = iota((toks, 2 * picked), 0)
    target = iota((toks, 2 * picked), 1) % picked * DILATION
    for h in range(heads):
        offset = lax.rem(lax.axis_index("head") * heads + h, DILATION)
        place = jnp.where(spot == target + offset, 1.0, 0.0).astype(BF16)
        wholes = []
        for column in (h, heads + h):
            mine = own_ref[:, cols(column)]
            upper = mine.astype(BF16)
            lower = (mine - upper.astype(F32)).astype(BF16)
            wholes.append(jnp.concatenate([upper, lower], axis=0))
        if h < early:
            parts = [
                (low, high, dkn_ref[low:high, cols(h)], dvn_ref[low:high, cols(h)])
                for low, high in blocks_of(toks)
            ]
        else:
            parts = near_backward(
                h, q_ref, k_ref, v_ref, p_ref, ds_ref, sc_ref, o_ref, dqf_ref, near_ref, dq_ref
            )
            send(h, 0, dq_ref, dq_hbm)
        for low, high, key_part, value_part in parts:
            rows = place[low:high]
            dk_ref[low:high, cols(h)] = (key_part + dot(rows, wholes[0])).astype(BF16)
            dv_ref[low:high, cols(h)] = (value_part + dot(rows, wholes[1])).astype(BF16)
        send(h, 1, dk_ref, dk_hbm)
        send(h, 2, dv_ref, dv_hbm)
    for copy in copies:
        copy.wait()


def shards(queries, keys, values, out_grad, norm_gain, doc_lengths, group_level):
    toks, width = queries.shape
    heads = width // HEAD_FEATURES
    ctx_size, head_size = lax.axis_size("ctx"), lax.axis_size("head")
    group_heads = heads * head_size // group_level.shape[0]
    picked = toks // DILATION
    reach = max(ctx_size // 2, 1)
    slots = reach + 1
    early = heads - heads // 4
    vmem = pl.BlockSpec(memory_space=pltpu.VMEM)
    hbm = pl.BlockSpec(memory_space=pltpu.HBM)
    far_parts = 1
    parts_back = 2 if heads % 2 == 0 else 1
    grads = jax.ShapeDtypeStruct((toks, width), BF16)
    across = (heads, HEAD_FEATURES, toks)
    held = (
        pltpu.VMEM((toks, width), BF16),
        pltpu.VMEM((toks, width), BF16),
        pltpu.VMEM((toks, early * HEAD_FEATURES), F32),
        pltpu.VMEM((toks, early * HEAD_FEATURES), F32),
        pltpu.VMEM((picked, 2 * width), F32),
        pltpu.VMEM((toks, width), BF16),
        pltpu.VMEM((toks, width), BF16),
        pltpu.VMEM((toks, width), BF16),
        pltpu.VMEM((heads, toks, toks), BF16),
        pltpu.VMEM(across, F32),
        pltpu.VMEM(across, F32),
        pltpu.VMEM(across, F32),
        pltpu.VMEM((heads, 1, toks), F32),
    )
    gain = norm_gain.reshape(1, width)
    operands = (queries, keys, values, out_grad, gain, doc_lengths, group_level)
    results = pl.pallas_call(
        functools.partial(kernel, ctx_size, head_size, reach, group_heads),
        out_shape=held,
        in_specs=[hbm] * 7,
        out_specs=(vmem,) * len(held),
        scratch_shapes=[
            pltpu.VMEM((far_parts, slots, picked, 2 * width // far_parts), BF16),
            pltpu.VMEM((parts_back, reach, picked, 2 * width // parts_back), BF16),
            pltpu.VMEM((parts_back, reach, picked, 2 * width // parts_back), BF16),
            pltpu.VMEM((8, toks), F32),
            pltpu.VMEM((head_size - 1, 8, toks), F32),
            pltpu.VMEM((toks, width), BF16),
            pltpu.VMEM((1, width), F32),
            pltpu.SMEM(doc_lengths.shape, jnp.int32),
            pltpu.SMEM(group_level.shape, jnp.int32),
            pltpu.SemaphoreType.DMA((7,)),
            pltpu.VMEM((toks, toks), F32),
            pltpu.VMEM((heads, slots * picked, toks), BF16),
            pltpu.VMEM((toks, toks), BF16),
            pltpu.SemaphoreType.DMA((far_parts, reach)),
            pltpu.SemaphoreType.DMA((far_parts, reach)),
            pltpu.SemaphoreType.DMA((parts_back, reach)),
            pltpu.SemaphoreType.DMA((parts_back, reach)),
            pltpu.SemaphoreType.DMA((head_size - 1,)),
            pltpu.SemaphoreType.DMA((head_size - 1,)),
        ],
        compiler_params=pltpu.CompilerParams(
            collective_id=0, has_side_effects=True, vmem_limit_bytes=32 * 1024 * 1024
        ),
    )(*(pltpu.with_memory_space_constraint(given, pltpu.HBM) for given in operands))
    return pl.pallas_call(
        finish,
        out_shape=(grads,) * 4,
        in_specs=[vmem] * len(held),
        out_specs=(hbm,) * 4,
        scratch_shapes=[
            pltpu.VMEM((toks, width), BF16),
            pltpu.VMEM((toks, width), BF16),
            pltpu.VMEM((toks, width), BF16),
            pltpu.VMEM((toks, toks), BF16),
            pltpu.SemaphoreType.DMA((1,)),
            pltpu.SemaphoreType.DMA((heads, 3)),
        ],
        compiler_params=pltpu.CompilerParams(vmem_limit_bytes=24 * 1024 * 1024),
    )(*results)


def solution(mesh):
    split = P("ctx", "head")
    return jax.shard_map(
        shards,
        mesh=mesh,
        in_specs=(split, split, split, split, P("head"), P(), P()),
        out_specs=(split, split, split, split),
        check_vma=False,
    )
```

```python
import functools
import math

import jax
import jax.numpy as jnp
from jax import lax
from jax.experimental import pallas as pl
from jax.experimental.pallas import tpu as pltpu
from jax.sharding import PartitionSpec as P

HEAD_FEATURES = 128
DILATION = 32
EPS = 1e-05
HIDDEN = -1e30
MESH = pl.DeviceIdType.MESH
F32 = jnp.float32
BF16 = jnp.bfloat16


def dot(a, b, left=1, right=0):
    return lax.dot_general(a, b, (((left,), (right,)), ((), ())), preferred_element_type=F32)


def iota(shape, dim):
    return lax.broadcasted_iota(jnp.int32, shape, dim)


def cols(h):
    return slice(h * HEAD_FEATURES, (h + 1) * HEAD_FEATURES)


def blocks_of(toks):
    return [(0, toks // 2), (toks // 2, toks)]


def near_backward(h, q_ref, k_ref, v_ref, p_ref, ds_ref, sc_ref, o_ref, dqf_ref, near_ref, dq_ref):
    toks = q_ref.shape[0]
    blocks = blocks_of(toks)
    scale = HEAD_FEATURES ** (-0.5)
    grad = (sc_ref[h] * near_ref[h]).astype(BF16)
    delta = jnp.sum(grad.astype(F32) * o_ref[h], axis=0, keepdims=True)
    keys_t = k_ref[:, cols(h)].T
    for low, high in blocks:
        product = dot(v_ref[0:high, cols(h)], grad[:, low:high])
        weight = p_ref[h, 0:high, low:high].astype(F32)
        slope = (weight * (product - delta[:, low:high])).astype(BF16)
        ds_ref[0:high, low:high] = slope
        query_grad = dot(keys_t[:, 0:high], slope) + dqf_ref[h, :, low:high]
        dq_ref[low:high, cols(h)] = (query_grad * scale).T.astype(BF16)
    return [
        (
            low,
            high,
            dot(ds_ref[low:high, low:toks], q_ref[low:toks, cols(h)]) * scale,
            dot(p_ref[h, low:high, low:toks], grad[:, low:toks], 1, 1),
        )
        for low, high in blocks
    ]


def kernel(
    ctx_size, head_size, reach, group_heads,
    q_hbm, k_hbm, v_hbm, og_hbm, gain_hbm, len_hbm, level_hbm,
    out_ref, dq_ref, dkn_ref, dvn_ref, own_ref,
    q_ref, k_ref, v_ref, p_ref, sc_ref, o_ref, dqf_ref, near_ref,
    far_ref, term_ref, back_ref, stat_ref, stats_ref,
    og_ref, gain_ref, len_ref, level_ref, load_sem,
    bias_ref, pf_ref, ds_ref,
    far_send, far_recv, back_send, back_recv, stat_send, stat_recv,
):
    loads = [
        pltpu.make_async_copy(source, target, load_sem.at[i])
        for i, (source, target) in enumerate(
            (
                (k_hbm, k_ref), (v_hbm, v_ref), (len_hbm, len_ref), (level_hbm, level_ref),
                (q_hbm, q_ref), (gain_hbm, gain_ref), (og_hbm, og_ref),
            )
        )
    ]
    for load in loads[:4]:
        load.start()
    toks, width = q_ref.shape
    heads = width // HEAD_FEATURES
    picked = toks // DILATION
    slots = reach + 1
    far_rows = slots * picked
    half = toks // 2
    early = dkn_ref.shape[1] // HEAD_FEATURES
    full = width * head_size
    scale = HEAD_FEATURES ** (-0.5)
    scale2 = scale * math.log2(math.e)
    c = lax.axis_index("ctx")
    hp = lax.axis_index("head")

    def wide_cols(h):
        return slice(width + h * HEAD_FEATURES, width + (h + 1) * HEAD_FEATURES)

    parts_back = back_ref.shape[0]
    part_heads = heads // parts_back
    far_parts = far_ref.shape[0]
    far_heads = heads // far_parts

    blocks = blocks_of(toks)

    barrier = pltpu.get_barrier_semaphore()
    for d in range(1, slots):
        @pl.when(c + d < ctx_size)
        def _():
            pl.semaphore_signal(barrier, inc=1, device_id=(c + d, hp), device_id_type=MESH)

        @pl.when(c >= d)
        def _():
            pl.semaphore_signal(barrier, inc=1, device_id=(c - d, hp), device_id_type=MESH)
    for e in range(1, head_size):
        peer = lax.rem(hp + e, head_size)
        pl.semaphore_signal(barrier, inc=1, device_id=(c, peer), device_id_type=MESH)

    for d in range(1, slots):
        @pl.when(c < d)
        def _():
            far_ref[:, d] = jnp.zeros((far_parts,) + far_ref.shape[2:], BF16)

        @pl.when(c + d >= ctx_size)
        def _():
            back_ref[:, d - 1] = jnp.zeros((parts_back,) + back_ref.shape[2:], BF16)

    loads[0].wait()
    loads[1].wait()
    for load in loads[4:]:
        load.start()

    def offset_of(h):
        return lax.rem(hp * heads + h, DILATION)

    row_of = iota((picked, toks), 0) * DILATION
    place_in = iota((picked, toks), 1)
    def pick_part(part):
        for spot in range(far_heads):
            h = part * far_heads + spot
            pick = jnp.where(place_in == row_of + offset_of(h), 1.0, 0.0).astype(BF16)
            far_ref[part, 0, :, cols(spot)] = dot(pick, k_ref[:, cols(h)]).astype(BF16)
            far_ref[part, 0, :, cols(spot + far_heads)] = dot(pick, v_ref[:, cols(h)]).astype(BF16)

    def far_rows_of(h):
        part, spot = divmod(h, far_heads)
        shape = (far_rows, HEAD_FEATURES)
        return (
            far_ref[part, :, :, cols(spot)].reshape(shape),
            far_ref[part, :, :, cols(spot + far_heads)].reshape(shape),
        )

    def far_copy(part, d):
        return pltpu.make_async_remote_copy(
            src_ref=far_ref.at[part, 0], dst_ref=far_ref.at[part, d],
            send_sem=far_send.at[part, d - 1], recv_sem=far_recv.at[part, d - 1],
            device_id=(c + d, hp), device_id_type=MESH,
        )

    before = jnp.minimum(c, reach)
    after = jnp.minimum(ctx_size - 1 - c, reach)
    for part in range(far_parts):
        pick_part(part)
        if part == 0:
            pl.semaphore_wait(barrier, before + after + (head_size - 1))
        for d in range(1, slots):
            @pl.when(c + d < ctx_size)
            def _():
                far_copy(part, d).start()

    def back_copy(part, d):
        return pltpu.make_async_remote_copy(
            src_ref=term_ref.at[part, d - 1], dst_ref=back_ref.at[part, d - 1],
            send_sem=back_send.at[part, d - 1], recv_sem=back_recv.at[part, d - 1],
            device_id=(c - d, hp), device_id_type=MESH,
        )

    def stat_copy(e):
        return pltpu.make_async_remote_copy(
            src_ref=stat_ref, dst_ref=stats_ref.at[e - 1],
            send_sem=stat_send.at[e - 1], recv_sem=stat_recv.at[e - 1],
            device_id=(c, lax.rem(hp + e, head_size)), device_id_type=MESH,
        )

    for load in loads[2:]:
        load.wait()

    place_q = iota((1, toks), 1) + c * toks
    first = jnp.zeros((1, toks), jnp.int32)
    end = jnp.int32(0)
    for i in range(len_ref.shape[0]):
        end = end + len_ref[i]
        first = jnp.maximum(first, jnp.where(place_q >= end, end, 0))
    for low, high in blocks:
        place_k = iota((high, half), 0) + c * toks
        seen = (place_k <= place_q[:, low:high]) & (place_k >= first[:, low:high])
        bias_ref[0:high, low:high] = jnp.where(seen, 0.0, HIDDEN)

    tops, sums = [], []
    scaled_sum = jnp.zeros((1, toks), F32)
    for h in range(heads):
        values_t = v_ref[:, cols(h)].T
        top_parts, sum_parts = [], []
        for low, high in blocks:
            logit = dot(k_ref[0:high, cols(h)], q_ref[low:high, cols(h)], 1, 1)
            logit = logit * scale2 + bias_ref[0:high, low:high]
            top = jnp.max(logit, axis=0, keepdims=True)
            weight = jnp.exp2(logit - top)
            top_parts.append(top)
            sum_parts.append(jnp.sum(weight, axis=0, keepdims=True))
            weight = weight.astype(BF16)
            p_ref[h, 0:high, low:high] = weight
            o_ref[h, :, low:high] = dot(values_t[:, 0:high], weight)
        tops.append(jnp.concatenate(top_parts, axis=1))
        sums.append(jnp.concatenate(sum_parts, axis=1))
        scaled = og_ref[:, cols(h)].astype(F32) * gain_ref[:, cols(h)]
        scaled = scaled.T
        sc_ref[h] = scaled
        scaled_sum = scaled_sum + jnp.sum(scaled, axis=0, keepdims=True)

    row = iota((far_rows, toks), 0)
    counter = (c - row // picked) * picked + row % picked
    near_scale, far_scale = [], []
    stats = [jnp.zeros((1, toks), F32) for _ in range(3)]
    for h in range(heads):
        if h % far_heads == 0:
            for d in range(1, slots):
                @pl.when(c >= d)
                def _():
                    far_copy(h // far_heads, d).wait_recv()
        far_k, far_v = far_rows_of(h)
        level = level_ref[(hp * heads + h) // group_heads]
        skip = jnp.left_shift(jnp.int32(1), level) - 1
        place_k = counter * DILATION + offset_of(h)
        seen = (place_k <= place_q) & (place_k >= first) & ((counter & skip) == 0)
        logit = jnp.where(seen, dot(far_k, q_ref[:, cols(h)], 1, 1) * scale2, HIDDEN)
        top = jnp.maximum(tops[h], jnp.max(logit, axis=0, keepdims=True))
        weight = jnp.exp2(logit - top)
        shrink = jnp.exp2(tops[h] - top)
        inverse = 1.0 / (sums[h] * shrink + jnp.sum(weight, axis=0, keepdims=True))
        weight = weight.astype(BF16)
        pf_ref[h] = weight
        near_scale.append(shrink * inverse)
        near_ref[h] = near_scale[h]
        far_scale.append(inverse)
        attended = (o_ref[h] * near_scale[h] + dot(far_v, weight, 0, 0) * inverse).astype(BF16)
        attended = attended.astype(F32)
        o_ref[h] = attended
        scaled = sc_ref[h]
        terms = (attended, attended * attended, scaled * attended)
        stats = [s + jnp.sum(t, axis=0, keepdims=True) for s, t in zip(stats, terms)]

    stats.append(scaled_sum)
    for i in range(4):
        stat_ref[i : i + 1, :] = stats[i]
    stat_ref[4:8, :] = jnp.zeros((4, toks), F32)
    for e in range(1, head_size):
        stat_copy(e).start()
    for e in range(1, head_size):
        stat_copy(e).wait_recv()
    total = stat_ref[...]
    for e in range(1, head_size):
        total = total + stats_ref[e - 1]
    total = total / full
    mean, square, cross, grad_mean = (total[i : i + 1, :] for i in range(4))
    rstd = lax.rsqrt(square - mean * mean + EPS)
    shift = -mean * rstd
    proj = rstd * (cross - mean * grad_mean)

    for h in range(heads):
        attended = o_ref[h]
        normed = attended * rstd + shift
        grad = rstd * (sc_ref[h] - grad_mean - normed * proj)
        sc_ref[h] = grad
        grad = (grad * far_scale[h]).astype(BF16)
        delta = jnp.sum(grad.astype(F32) * attended, axis=0, keepdims=True)
        far_v = far_rows_of(h)[1]
        weight = pf_ref[h]
        slope = (weight.astype(F32) * (dot(far_v, grad) - delta)).astype(BF16)
        key_term = dot(slope, q_ref[:, cols(h)]) * scale
        value_term = dot(weight, grad, 1, 1)
        pf_ref[h] = slope
        own_ref[:, cols(h)] = key_term[0:picked]
        own_ref[:, wide_cols(h)] = value_term[0:picked]
        part, spot = divmod(h, part_heads)
        term_ref[part, :, :, cols(spot)] = (
            key_term[picked:].astype(BF16).reshape(reach, picked, HEAD_FEATURES)
        )
        term_ref[part, :, :, cols(spot + part_heads)] = (
            value_term[picked:].astype(BF16).reshape(reach, picked, HEAD_FEATURES)
        )
        if spot == part_heads - 1:
            for d in reversed(range(1, slots)):
                @pl.when(c >= d)
                def _():
                    back_copy(part, d).start()

    for h in range(heads):
        dqf_ref[h] = dot(far_rows_of(h)[0], pf_ref[h], 0, 0)
        normed = o_ref[h] * rstd + shift
        out_ref[:, cols(h)] = (normed.T * gain_ref[:, cols(h)]).astype(BF16)

    for h in range(early):
        for low, high, key_part, value_part in near_backward(
            h, q_ref, k_ref, v_ref, p_ref, ds_ref, sc_ref, o_ref, dqf_ref, near_ref, dq_ref
        ):
            dkn_ref[low:high, cols(h)] = key_part
            dvn_ref[low:high, cols(h)] = value_part

    for part in range(parts_back):
        for d in range(1, slots):
            @pl.when(c + d < ctx_size)
            def _():
                back_copy(part, d).wait_recv()
        theirs = back_ref[part, 0].astype(F32)
        for d in range(2, slots):
            theirs = theirs + back_ref[part, d - 1].astype(F32)
        for inner in range(part_heads):
            h = part * part_heads + inner
            own_ref[:, cols(h)] = own_ref[:, cols(h)] + theirs[:, cols(inner)]
            own_ref[:, wide_cols(h)] = (
                own_ref[:, wide_cols(h)] + theirs[:, cols(inner + part_heads)]
            )

    for d in range(1, slots):
        @pl.when(c + d < ctx_size)
        def _():
            for part in range(far_parts):
                far_copy(part, d).wait_send()

        @pl.when(c >= d)
        def _():
            for part in range(parts_back):
                back_copy(part, d).wait_send()
    for e in range(1, head_size):
        stat_copy(e).wait_send()


def finish(
    out_ref, dqe_ref, dkn_ref, dvn_ref, own_ref,
    q_ref, k_ref, v_ref, p_ref, sc_ref, o_ref, dqf_ref, near_ref,
    out_hbm, dq_hbm, dk_hbm, dv_hbm,
    dq_ref, dk_ref, dv_ref, ds_ref, out_sem, head_sem,
):
    toks, width = q_ref.shape
    heads = width // HEAD_FEATURES
    picked = own_ref.shape[0]
    early = dkn_ref.shape[1] // HEAD_FEATURES
    copies = [pltpu.make_async_copy(out_ref, out_hbm, out_sem.at[0])]
    copies[0].start()

    def send(h, i, source, target):
        copy = pltpu.make_async_copy(
            source.at[:, cols(h)], target.at[:, cols(h)], head_sem.at[h, i]
        )
        copy.start()
        copies.append(copy)

    for h in range(early):
        send(h, 0, dqe_ref, dq_hbm)
    spot = iota((toks, 2 * picked), 0)
    target = iota((toks, 2 * picked), 1) % picked * DILATION
    for h in range(heads):
        offset = lax.rem(lax.axis_index("head") * heads + h, DILATION)
        place = jnp.where(spot == target + offset, 1.0, 0.0).astype(BF16)
        wholes = []
        for column in (h, heads + h):
            mine = own_ref[:, cols(column)]
            upper = mine.astype(BF16)
            lower = (mine - upper.astype(F32)).astype(BF16)
            wholes.append(jnp.concatenate([upper, lower], axis=0))
        if h < early:
            parts = [
                (low, high, dkn_ref[low:high, cols(h)], dvn_ref[low:high, cols(h)])
                for low, high in blocks_of(toks)
            ]
        else:
            parts = near_backward(
                h, q_ref, k_ref, v_ref, p_ref, ds_ref, sc_ref, o_ref, dqf_ref, near_ref, dq_ref
            )
            send(h, 0, dq_ref, dq_hbm)
        for low, high, key_part, value_part in parts:
            rows = place[low:high]
            dk_ref[low:high, cols(h)] = (key_part + dot(rows, wholes[0])).astype(BF16)
            dv_ref[low:high, cols(h)] = (value_part + dot(rows, wholes[1])).astype(BF16)
        send(h, 1, dk_ref, dk_hbm)
        send(h, 2, dv_ref, dv_hbm)
    for copy in copies:
        copy.wait()


def shards(queries, keys, values, out_grad, norm_gain, doc_lengths, group_level):
    toks, width = queries.shape
    heads = width // HEAD_FEATURES
    ctx_size, head_size = lax.axis_size("ctx"), lax.axis_size("head")
    group_heads = heads * head_size // group_level.shape[0]
    picked = toks // DILATION
    reach = max(ctx_size // 2, 1)
    slots = reach + 1
    early = heads - heads // 4
    vmem = pl.BlockSpec(memory_space=pltpu.VMEM)
    hbm = pl.BlockSpec(memory_space=pltpu.HBM)
    far_parts = 1
    parts_back = 1
    grads = jax.ShapeDtypeStruct((toks, width), BF16)
    across = (heads, HEAD_FEATURES, toks)
    held = (
        pltpu.VMEM((toks, width), BF16),
        pltpu.VMEM((toks, width), BF16),
        pltpu.VMEM((toks, early * HEAD_FEATURES), F32),
        pltpu.VMEM((toks, early * HEAD_FEATURES), F32),
        pltpu.VMEM((picked, 2 * width), F32),
        pltpu.VMEM((toks, width), BF16),
        pltpu.VMEM((toks, width), BF16),
        pltpu.VMEM((toks, width), BF16),
        pltpu.VMEM((heads, toks, toks), BF16),
        pltpu.VMEM(across, F32),
        pltpu.VMEM(across, F32),
        pltpu.VMEM(across, F32),
        pltpu.VMEM((heads, 1, toks), F32),
    )
    gain = norm_gain.reshape(1, width)
    operands = (queries, keys, values, out_grad, gain, doc_lengths, group_level)
    results = pl.pallas_call(
        functools.partial(kernel, ctx_size, head_size, reach, group_heads),
        out_shape=held,
        in_specs=[hbm] * 7,
        out_specs=(vmem,) * len(held),
        scratch_shapes=[
            pltpu.VMEM((far_parts, slots, picked, 2 * width // far_parts), BF16),
            pltpu.VMEM((parts_back, reach, picked, 2 * width // parts_back), BF16),
            pltpu.VMEM((parts_back, reach, picked, 2 * width // parts_back), BF16),
            pltpu.VMEM((8, toks), F32),
            pltpu.VMEM((head_size - 1, 8, toks), F32),
            pltpu.VMEM((toks, width), BF16),
            pltpu.VMEM((1, width), F32),
            pltpu.SMEM(doc_lengths.shape, jnp.int32),
            pltpu.SMEM(group_level.shape, jnp.int32),
            pltpu.SemaphoreType.DMA((7,)),
            pltpu.VMEM((toks, toks), F32),
            pltpu.VMEM((heads, slots * picked, toks), BF16),
            pltpu.VMEM((toks, toks), BF16),
            pltpu.SemaphoreType.DMA((far_parts, reach)),
            pltpu.SemaphoreType.DMA((far_parts, reach)),
            pltpu.SemaphoreType.DMA((parts_back, reach)),
            pltpu.SemaphoreType.DMA((parts_back, reach)),
            pltpu.SemaphoreType.DMA((head_size - 1,)),
            pltpu.SemaphoreType.DMA((head_size - 1,)),
        ],
        compiler_params=pltpu.CompilerParams(
            collective_id=0, has_side_effects=True, vmem_limit_bytes=32 * 1024 * 1024
        ),
    )(*(pltpu.with_memory_space_constraint(given, pltpu.HBM) for given in operands))
    return pl.pallas_call(
        finish,
        out_shape=(grads,) * 4,
        in_specs=[vmem] * len(held),
        out_specs=(hbm,) * 4,
        scratch_shapes=[
            pltpu.VMEM((toks, width), BF16),
            pltpu.VMEM((toks, width), BF16),
            pltpu.VMEM((toks, width), BF16),
            pltpu.VMEM((toks, toks), BF16),
            pltpu.SemaphoreType.DMA((1,)),
            pltpu.SemaphoreType.DMA((heads, 3)),
        ],
        compiler_params=pltpu.CompilerParams(vmem_limit_bytes=24 * 1024 * 1024),
    )(*results)


def solution(mesh):
    split = P("ctx", "head")
    return jax.shard_map(
        shards,
        mesh=mesh,
        in_specs=(split, split, split, split, P("head"), P(), P()),
        out_specs=(split, split, split, split),
        check_vma=False,
    )
```
